1024 devices in a mesh: dp: 8 (over x, core), node: 16 (over z_lo), local: 8 (over y, z_hi).
Axes of the slice: x: 4, y: 4, z: 32 (z_hi: 2, z_lo: 16; z = z_hi * 16 + z_lo), core: 2. Of those that a mesh axis runs over, the one named last changes fastest.
Arguments:
- grad_out: bfloat16 [16384, 2048], P(('dp', 'node', 'local')), may hold values from -6 to 6
- saved_pre: bfloat16 [16384, 8, 1536], P(('dp', 'node', 'local')), may hold values from -6 to 6
- gates: float32 [16384, 8], P(('dp', 'node', 'local')), may hold values from 0.1 to 1
- routes: int32 [16384, 8], P(('dp', 'node', 'local')), may hold values from 0 to 127, all different within a row; in each aligned block of 16 rows (0 to 15, 16 to 31, ...) at most 2 rows name the same one
- w_gate: bfloat16 [128, 2048, 768], P(('node', 'local')), may hold values from -0.125 to 0.125
- w_up: bfloat16 [128, 2048, 768], P(('node', 'local')), may hold values from -0.125 to 0.125
- w_down: bfloat16 [128, 768, 2048], P(('node', 'local')), may hold values from -0.21875 to 0.21875
Outputs:
- d_tokens: bfloat16 [16384, 2048], P(('dp', 'node', 'local'))
- d_gates: float32 [16384, 8], P(('dp', 'node', 'local'))
- d_down: bfloat16 [128, 768, 2048], P(('node', 'local'), 'dp')
The draws below stay inside these ranges and needn't reach their ends.
Inputs may be any that keep to these rules, and one draw needn't show every extreme that they name: `routes`: within the rows of one device (aligned blocks of 16 tokens) no expert is named by more than 2 tokens, a bound that some block reaches.
All inputs are finite; a program needn't handle non-finite values.
Results may differ from the reference program's by a relative error of at most 0.017.
Values may be sent and summed in bfloat16 or wider, within the bound.
No kernel may reach another device: no remote copies, remote signals or barrier semaphores. Data moves between devices by JAX's collectives and lax.ppermute only.
A program may use at most 64 MiB of HBM per device.

```python
import math
import jax
import jax.numpy as jnp
import numpy as np
from jax import lax

D = 2048
F = 768
TOPK = 8
TOK_DEV = 16
EXPERTS = 128
CAP = 2
TOKENS = 16384
N_DP = 8


def steps_of(own_key, extent, split, least, top_value):
    def one(axis_at, shards_of):
        draws = jax.random.uniform(jax.random.fold_in(jax.random.fold_in(own_key, 6), axis_at), (shards_of,), jnp.float32, least / len(split), top_value / len(split))
        return jnp.repeat(jnp.exp(draws), extent[axis_at] // shards_of).reshape((-1,) + (1,) * (len(extent) - axis_at - 1))

    level = one(*split[0])
    for cut in split[1:]:
        level = level * one(*cut)
    return level


def deal_out(rng, own, number, rows, count, top, limit, slope):
    ranking = jax.random.permutation(rng, count)
    heavy_load, common = load_shares(count, rows * top, limit, slope, True), load_shares(count, rows * top, limit, slope, False)
    places = jnp.arange(count)

    def named(sizes, turn):
        used = int((sizes > 0).sum())
        fixed = max(1, used // 4)
        moved = fixed + (places - fixed + turn * (used - fixed)) % max(1, count - fixed)
        return jnp.zeros((count,), jnp.int32).at[ranking[jnp.where(places < fixed, places, moved)]].set(jnp.asarray(sizes, jnp.int32))

    sizes = jnp.where(number % 4 == 0, named(heavy_load, number // 4), named(common, number - number // 4 - 1))
    mixed = jax.random.permutation(jax.random.fold_in(own, 3), count)
    source_of, sink = mixed[0:count // 2 * 2:2], mixed[1:count // 2 * 2:2]
    slack = jnp.minimum(sizes[source_of] - 1, limit - sizes[sink]) // 2
    slack = jnp.where((source_of == ranking[0]) | (sink == ranking[0]) | (sizes[sink] == 0), 0, jnp.maximum(slack, 0))
    moved = jax.random.randint(jax.random.fold_in(own, 4), (count // 2,), 0, 1 << 20) % (slack + 1)
    sizes = sizes.at[source_of].add(-moved).at[sink].add(moved)
    labels = jnp.searchsorted(jnp.cumsum(sizes), jnp.arange(rows * top), side="right").astype(jnp.int32)
    table = labels.reshape(top, rows).T
    table = table[jax.random.permutation(jax.random.fold_in(own, 1), rows)]
    turn = jax.random.randint(jax.random.fold_in(own, 2), (rows, 1), 0, top)
    return jnp.take_along_axis(table, (jnp.arange(top)[None, :] + turn) % top, axis=1)


def load_shares(amount, total, reach, skew, full):
    portions = [(1 << 20) // math.isqrt(standing ** skew) + 1 for standing in range(1, amount + 1)]
    largest = reach if full else min(reach, max(-(-total // amount), total * portions[0] // sum(portions)))
    least = 1 if total - largest >= amount - 1 else 0
    given, spare = [largest] + [least] * (amount - 1), total - largest - least * (amount - 1)
    while spare > 0:
        candidates = [i for i in range(1, amount) if given[i] < largest] or [i for i in range(1, amount) if given[i] < reach]
        mass, left = sum([portions[i] for i in candidates]), spare
        for i in candidates:
            more = min(reach - given[i], max(1, left * portions[i] // mass), spare)
            given[i] = given[i] + more
            spare = spare - more
    return np.array(given)


def noise(stream_key, shape, scale, limit, cuts=(), held_as=jnp.bfloat16):
    result = jax.random.normal(stream_key, shape, jnp.float32) * scale
    if len(cuts) > 0:
        result = steps_of(stream_key, shape, cuts, -0.22, 0.18) * result
    return jnp.clip(result, min=-limit, max=limit).astype(held_as)


def setup_inputs(seed: int = 0) -> dict:
    key_of = jax.random.split(jax.random.key(seed), 8)
    grad_out = noise(key_of[0], (TOKENS, D), 1.0, 6.0, ((0, 1024),))
    saved_pre = noise(key_of[1], (TOKENS, TOPK, 2 * F), 1.0, 6.0, ((0, 1024),))
    gates = jnp.clip(0.1 + 0.9 * jax.random.uniform(key_of[2], (TOKENS, TOPK), jnp.float32) ** steps_of(key_of[2], (TOKENS, TOPK), ((0, 1024),), -0.2, 0.2), 0.1, 1.0)
    routes_keys = jax.random.split(jax.random.fold_in(key_of[3], 1), TOKENS // TOK_DEV)
    routes_turns = jax.random.permutation(jax.random.fold_in(key_of[3], 3), TOKENS // TOK_DEV)
    routes = jax.vmap(lambda own, number: deal_out(jax.random.fold_in(key_of[3], 2), own, number, TOK_DEV, EXPERTS, TOPK, CAP, 2))(routes_keys, routes_turns).reshape((TOKENS, TOPK))
    w_gate = noise(key_of[4], (EXPERTS, D, F), D ** -0.5, 0.125, ((0, 128),))
    w_up = noise(key_of[5], (EXPERTS, D, F), D ** -0.5, 0.125, ((0, 128),))
    w_down = noise(key_of[6], (EXPERTS, F, D), F ** -0.5, 0.21875, ((0, 128),))
    return {"grad_out": grad_out, "saved_pre": saved_pre, "gates": gates, "routes": routes, "w_gate": w_gate, "w_up": w_up, "w_down": w_down}


def expert_rows(weight_rows, pre_rows, gate_weight, up_weight, down_weight):
    hidden_width = down_weight.shape[0]
    gate_pre = pre_rows[:, :hidden_width].astype(jnp.float32)
    up_pre = pre_rows[:, hidden_width:].astype(jnp.float32)
    sigmoid_gate = jax.nn.sigmoid(gate_pre)
    activated = gate_pre * sigmoid_gate
    hidden = (activated * up_pre).astype(jnp.bfloat16)
    hidden_grad = lax.dot_general(weight_rows, down_weight, (((1,), (1,)), ((), ())), preferred_element_type=jnp.float32)
    gate_dots = jnp.sum(hidden.astype(jnp.float32) * hidden_grad, axis=1).astype(jnp.bfloat16)
    gate_grad = (hidden_grad * up_pre * sigmoid_gate * (1.0 + gate_pre * (1.0 - sigmoid_gate))).astype(jnp.bfloat16)
    up_grad = (hidden_grad * activated).astype(jnp.bfloat16)
    contract = (((1,), (1,)), ((), ()))
    route_grad = lax.dot_general(gate_grad, gate_weight, contract, preferred_element_type=jnp.float32)
    route_grad = route_grad + lax.dot_general(up_grad, up_weight, contract, preferred_element_type=jnp.float32)
    return hidden, route_grad.astype(jnp.bfloat16), gate_dots


def expert_step(operands):
    weight_rows, pre_rows, gate_weight, up_weight, down_weight = operands
    hidden, route_grad, gate_dots = expert_rows(weight_rows, pre_rows, gate_weight, up_weight, down_weight)
    partial_sum = lax.dot_general(hidden, weight_rows, (((0,), (0,)), ((), ())), preferred_element_type=jnp.float32)
    return route_grad, gate_dots, partial_sum.astype(jnp.bfloat16)


def reference(grad_out, saved_pre, gates, routes, w_gate, w_up, w_down):
    route_count = TOK_DEV * TOPK
    slot_count = EXPERTS * CAP
    grad_blocks = grad_out.reshape(N_DP, EXPERTS, TOK_DEV, D)
    pre_blocks = saved_pre.reshape(N_DP, EXPERTS, route_count, 2 * F)
    gate_blocks = gates.reshape(N_DP, EXPERTS, TOK_DEV, TOPK)
    route_blocks = routes.reshape(N_DP, EXPERTS, route_count)
    expert_iota = jnp.arange(EXPERTS, dtype=jnp.int32)

    def replica(running, operands):
        grad_block, pre_block, gate_block, route_block = operands
        weighted = (gate_block[..., None] * grad_block[:, :, None, :].astype(jnp.float32)).astype(jnp.bfloat16)
        weighted = weighted.reshape(EXPERTS * route_count, D)
        onehot = (route_block[..., None] == expert_iota).astype(jnp.int32)
        within = jnp.sum(jnp.cumsum(onehot, axis=1) * onehot, axis=2) - 1
        target = (route_block * slot_count + expert_iota[:, None] * CAP + within).reshape(-1).astype(jnp.int32)
        send_weighted = jnp.zeros((EXPERTS * slot_count, D), jnp.bfloat16).at[target].set(weighted)
        send_pre = jnp.zeros((EXPERTS * slot_count, 2 * F), jnp.bfloat16).at[target].set(pre_block.reshape(-1, 2 * F))
        route_grad, gate_dots, partials = lax.map(expert_step, (send_weighted.reshape(EXPERTS, slot_count, D), send_pre.reshape(EXPERTS, slot_count, 2 * F), w_gate, w_up, w_down))
        returned = route_grad.reshape(-1, D)[target].reshape(EXPERTS, TOK_DEV, TOPK, D)
        token_grad = jnp.sum(returned.astype(jnp.float32), axis=2).astype(jnp.bfloat16)
        score_grad = gate_dots.reshape(-1)[target].reshape(EXPERTS, TOK_DEV, TOPK).astype(jnp.float32) / gate_block
        return running + partials.astype(jnp.float32), (token_grad, score_grad)

    running, outputs = lax.scan(replica, jnp.zeros((EXPERTS, F, D), jnp.float32), (grad_blocks, pre_blocks, gate_blocks, route_blocks))
    token_grads, score_grads = outputs
    return token_grads.reshape(TOKENS, D), score_grads.reshape(TOKENS, TOPK), running.astype(jnp.bfloat16)
```

```python
import jax
import jax.numpy as jnp
from jax import lax
from jax.sharding import Mesh, PartitionSpec as P

RING = ("node", "zh")
CAP = 2


def dot_rows(left, right, contract):
    return lax.dot_general(left, right, ((contract[:1], contract[1:]), ((), ())), preferred_element_type=jnp.float32)


def expert_of(ring_index, column):
    return (ring_index // 2) * 8 + column * 2 + ring_index % 2


def slot_masks(routes, experts):
    named = routes[..., None] == experts
    hits = jnp.any(named, axis=-2)
    counts = hits.astype(jnp.int32)
    before = jnp.cumsum(counts, axis=-2) - counts
    taken = hits[..., None] & (before[..., None] == jnp.arange(CAP, dtype=jnp.int32))
    return named, taken


def shards(grad_out, saved_pre, gates, routes, w_gate, w_up, w_down):
    tok, topk = routes.shape
    width = grad_out.shape[1]
    pre_width = saved_pre.shape[2]
    hidden_width = pre_width // 2
    ring = lax.axis_size("node") * lax.axis_size("zh")
    cols = lax.axis_size("y")
    me_y = lax.axis_index("y")
    f32, bf16 = jnp.float32, jnp.bfloat16
    ring_at = jnp.arange(ring, dtype=jnp.int32)

    gate_hi = lax.reduce_precision(gates, 8, 7)
    gate_mid = lax.reduce_precision(gates - gate_hi, 8, 7)
    gate_low = gates - gate_hi - gate_mid
    facts = jnp.concatenate([routes.astype(f32), gate_hi, gate_mid, gate_low], axis=1).astype(bf16)
    facts = jnp.pad(facts, ((0, 0), (0, 128 - 4 * topk)))
    payload = jnp.concatenate([grad_out, facts], axis=1)
    payload = jnp.broadcast_to(payload[None], (cols,) + payload.shape)
    column = lax.all_to_all(payload, "y", 0, 0, tiled=True)
    grad_col = column[:, :, :width].reshape(cols * tok, width)
    facts = column[:, :, width : width + 4 * topk].astype(f32)
    routes_col = facts[:, :, :topk].astype(jnp.int32)
    gates_col = facts[:, :, topk : 2 * topk] + facts[:, :, 2 * topk : 3 * topk] + facts[:, :, 3 * topk :]

    all_experts = expert_of(ring_at[None, :], jnp.arange(cols, dtype=jnp.int32)[:, None]).reshape(-1)
    named, taken = slot_masks(routes, all_experts)
    pick = named[..., None] & taken[:, None]
    pick = pick.reshape(tok * topk, cols * ring * CAP).astype(bf16)
    send_pre = dot_rows(pick, saved_pre.reshape(tok * topk, pre_width), (0, 0)).astype(bf16)
    pre_col = lax.all_to_all(send_pre.reshape(cols, ring * CAP, pre_width), "y", 0, 0, tiled=True)
    slots = cols * ring * CAP
    at = jnp.arange(slots, dtype=jnp.int32)
    origin = (at // CAP % cols) * (ring * CAP) + (at // (CAP * cols)) * CAP + at % CAP
    swap = (origin[:, None] == at[None, :]).astype(bf16)
    pre_ring = dot_rows(swap, pre_col.reshape(slots, pre_width), (1, 0)).astype(bf16)
    pre_ring = pre_ring.reshape(ring, cols * CAP, pre_width)

    mine = expert_of(ring_at, me_y)
    named_col, taken_col = slot_masks(routes_col, mine)
    gate_tok = jnp.sum(jnp.where(named_col, gates_col[..., None], 0.0), axis=2)
    gate_slot = jnp.sum(jnp.where(taken_col, gate_tok[..., None], 0.0), axis=1)
    gate_slot = gate_slot.transpose(1, 0, 2).reshape(slots, 1)
    same_col = jnp.arange(cols)[:, None] == jnp.arange(cols)[None, :]
    place = taken_col.transpose(2, 0, 3, 1)[:, :, :, None, :] & same_col[None, :, None, :, None]
    place = place.reshape(slots, cols * tok).astype(bf16)
    send_weighted = (dot_rows(place, grad_col, (1, 0)) * gate_slot).astype(bf16)
    send_weighted = send_weighted.reshape(ring, cols * CAP, width)

    weight_rows = lax.all_to_all(send_weighted, RING, 0, 0, tiled=True).reshape(slots, width)
    pre_rows = lax.all_to_all(pre_ring, RING, 0, 0, tiled=True).reshape(slots, pre_width)

    gate_pre = pre_rows[:, :hidden_width].astype(f32)
    up_pre = pre_rows[:, hidden_width:].astype(f32)
    sigmoid_gate = jax.nn.sigmoid(gate_pre)
    activated = gate_pre * sigmoid_gate
    hidden = (activated * up_pre).astype(bf16)
    partial = dot_rows(hidden, weight_rows, (0, 0)).astype(bf16)
    hidden_grad = dot_rows(weight_rows, w_down[0], (1, 1))
    gate_dots = jnp.sum(hidden.astype(f32) * hidden_grad, axis=1, keepdims=True).astype(bf16)
    gate_grad = (hidden_grad * up_pre * sigmoid_gate * (1.0 + gate_pre * (1.0 - sigmoid_gate))).astype(bf16)
    up_grad = (hidden_grad * activated).astype(bf16)
    d_down = lax.psum_scatter(partial, "dp", scatter_dimension=0, tiled=True)
    route_grad = dot_rows(gate_grad, w_gate[0], (1, 1)) + dot_rows(up_grad, w_up[0], (1, 1))
    back = jnp.concatenate([route_grad.astype(bf16), jnp.pad(gate_dots, ((0, 0), (0, 127)))], axis=1)
    back = lax.all_to_all(back.reshape(ring, cols * CAP, width + 128), RING, 0, 0, tiled=True)
    back = back.reshape(slots, width + 128)

    token_part = dot_rows(place, back[:, :width], (0, 0))
    dots = back[:, width].astype(f32).reshape(ring, cols, CAP).transpose(1, 0, 2)
    dots_tok = jnp.sum(jnp.where(taken_col, dots[:, None], 0.0), axis=3)
    dots_route = jnp.sum(jnp.where(named_col, dots_tok[:, :, None], 0.0), axis=3)
    dots_route = jnp.pad(dots_route.reshape(cols * tok, topk), ((0, 0), (0, 128 - topk)))
    home = jnp.concatenate([token_part, dots_route], axis=1).astype(bf16)
    home = lax.all_to_all(home.reshape(cols, tok, width + 128), "y", 0, 0, tiled=True)
    total = jnp.sum(home.astype(f32), axis=0)
    d_tokens = total[:, :width].astype(bf16)
    d_gates = total[:, width : width + topk] / gates
    return (d_tokens, d_gates, d_down[None])


def solution(mesh):
    devices = mesh.devices
    dp, node, local = devices.shape
    split = Mesh(devices.reshape(dp, node, local // 2, 2), ("dp", "node", "y", "zh"))
    owner = ("dp", "node", "y", "zh")
    expert = ("node", "y", "zh")
    in_specs = (
        P(owner, None),
        P(owner, None, None),
        P(owner, None),
        P(owner, None),
        P(expert, None, None),
        P(expert, None, None),
        P(expert, None, None),
    )
    out_specs = (P(owner, None), P(owner, None), P(expert, "dp", None))
    return jax.shard_map(shards, mesh=split, in_specs=in_specs, out_specs=out_specs, check_vma=False)
```

```python
import jax
import jax.numpy as jnp
from jax import lax
from jax.sharding import Mesh, PartitionSpec as P

RING = ("node", "zh")
CAP = 2
RING_SIZE = 32
HALF = RING_SIZE // 2
REACH = 5
LEAP = 2 * REACH + 1


def dot_rows(left, right, contract):
    return lax.dot_general(left, right, ((contract[:1], contract[1:]), ((), ())), preferred_element_type=jnp.float32)


def ring_index(place):
    return (place % HALF) * 2 + place // HALF


def expert_of(place, column):
    return (place % HALF) * 8 + column * 2 + place // HALF


def shift(value, hops):
    pairs = [(ring_index(place), ring_index((place + hops) % RING_SIZE)) for place in range(RING_SIZE)]
    return lax.ppermute(value, RING, pairs)


def slot_masks(routes, experts):
    named = routes[..., None] == experts
    hits = jnp.any(named, axis=-2)
    counts = hits.astype(jnp.int32)
    before = jnp.cumsum(counts, axis=-2) - counts
    taken = hits[..., None] & (before[..., None] == jnp.arange(CAP, dtype=jnp.int32))
    return named, taken


def shards(grad_out, saved_pre, gates, routes, w_gate, w_up, w_down):
    tok, topk = routes.shape
    width = grad_out.shape[1]
    pre_width = saved_pre.shape[2]
    hidden_width = pre_width // 2
    ring = RING_SIZE
    cols = lax.axis_size("y")
    me_y = lax.axis_index("y")
    me_z = lax.axis_index("zh") * HALF + lax.axis_index("node")
    f32, bf16 = jnp.float32, jnp.bfloat16
    leaps = jnp.array([0, LEAP, -LEAP], jnp.int32)
    steps = jnp.arange(-REACH, REACH + 1, dtype=jnp.int32)
    hubs = 3
    spread = LEAP
    order = [d for r in range(1, REACH + 1) for d in (r, -r)]

    gate_hi = lax.reduce_precision(gates, 8, 7)
    gate_mid = lax.reduce_precision(gates - gate_hi, 8, 7)
    gate_low = gates - gate_hi - gate_mid
    facts = jnp.concatenate([routes.astype(f32), gate_hi, gate_mid, gate_low], axis=1).astype(bf16)
    facts = jnp.pad(facts, ((0, 0), (0, 128 - 4 * topk)))
    payload = jnp.concatenate([grad_out, facts], axis=1)
    held = jnp.stack([payload, shift(payload, LEAP), shift(payload, -LEAP)])

    ring_at = jnp.arange(ring, dtype=jnp.int32)
    place_of = ring_at % 2 * HALF + ring_at // 2
    all_experts = expert_of(place_of[None, :], jnp.arange(cols, dtype=jnp.int32)[:, None]).reshape(-1)
    named, taken = slot_masks(routes, all_experts)
    pick = named[..., None] & taken[:, None]
    pick = pick.reshape(tok * topk, cols * ring * CAP).astype(bf16)
    send_pre = dot_rows(pick, saved_pre.reshape(tok * topk, pre_width), (0, 0)).astype(bf16)
    pre_col = lax.all_to_all(send_pre.reshape(cols, ring * CAP, pre_width), "y", 0, 0, tiled=True)
    slots = cols * ring * CAP
    at = jnp.arange(slots, dtype=jnp.int32)
    origin = (at // CAP % cols) * (ring * CAP) + (at // (CAP * cols)) * CAP + at % CAP
    swap = (origin[:, None] == at[None, :]).astype(bf16)
    pre_ring = dot_rows(swap, pre_col.reshape(slots, pre_width), (1, 0)).astype(bf16)
    pre_ring = pre_ring.reshape(ring, cols * CAP, pre_width)

    column = jnp.broadcast_to(held.reshape(1, hubs * tok, width + 128), (cols, hubs * tok, width + 128))
    column = lax.all_to_all(column, "y", 0, 0, tiled=True)
    column, pre_ring = lax.optimization_barrier((column, pre_ring))
    pre_rows = lax.all_to_all(pre_ring, RING, 0, 0, tiled=True).reshape(slots, pre_width)

    grad_col = column[:, :, :width].reshape(cols * hubs * tok, width)
    facts = column[:, :, width : width + 4 * topk].astype(f32).reshape(cols, hubs, tok, 4 * topk)
    routes_col = facts[..., :topk].astype(jnp.int32)
    gates_col = facts[..., topk : 2 * topk] + facts[..., 2 * topk : 3 * topk] + facts[..., 3 * topk :]

    mine = expert_of((me_z + steps) % ring, me_y)
    named_col, taken_col = slot_masks(routes_col, mine)
    serves = ~((leaps[:, None] == -LEAP) & (steps[None, :] == -REACH))
    taken_col = taken_col & serves[None, :, None, :, None]
    gate_tok = jnp.sum(jnp.where(named_col, gates_col[..., None], 0.0), axis=3)
    gate_slot = jnp.sum(jnp.where(taken_col, gate_tok[..., None], 0.0), axis=2)
    rows = spread * hubs * cols * CAP
    block = hubs * cols * CAP
    gate_slot = gate_slot.transpose(2, 1, 0, 3).reshape(rows, 1)
    same_col = jnp.arange(cols)[:, None] == jnp.arange(cols)[None, :]
    same_hub = jnp.arange(hubs)[:, None] == jnp.arange(hubs)[None, :]
    same = same_hub[:, None, None, None, :] & same_col[None, :, None, :, None]
    place = taken_col.transpose(3, 1, 0, 4, 2)[:, :, :, :, None, None, :] & same[None, ..., None]
    place = place.reshape(rows, cols * hubs * tok).astype(bf16)
    weighted = (dot_rows(place, grad_col, (1, 0)) * gate_slot).astype(bf16)
    arrived = {0: weighted[REACH * block : (REACH + 1) * block]}
    for d in order:
        arrived[d] = shift(weighted[(d + REACH) * block : (d + REACH + 1) * block], d)
    weight_rows = jnp.concatenate([arrived[d] for d in range(-REACH, REACH + 1)], axis=0)

    from_place = (me_z - steps[:, None] - leaps[None, :]) % ring
    from_row = ring_index(from_place)[:, :, None] * (cols * CAP) + jnp.arange(cols * CAP, dtype=jnp.int32)
    from_row = jnp.where(serves.T[:, :, None], from_row, -1).reshape(rows)
    turn = (from_row[:, None] == at[None, :]).astype(bf16)
    pre = dot_rows(turn, pre_rows, (1, 0))
    gate_pre = pre[:, :hidden_width]
    up_pre = pre[:, hidden_width:]
    sigmoid_gate = jax.nn.sigmoid(gate_pre)
    activated = gate_pre * sigmoid_gate
    hidden = (activated * up_pre).astype(bf16)
    partial = dot_rows(hidden, weight_rows, (0, 0)).astype(bf16)
    hidden_grad = dot_rows(weight_rows, w_down[0], (1, 1))
    gate_dots = jnp.sum(hidden.astype(f32) * hidden_grad, axis=1, keepdims=True).astype(bf16)
    gate_grad = (hidden_grad * up_pre * sigmoid_gate * (1.0 + gate_pre * (1.0 - sigmoid_gate))).astype(bf16)
    up_grad = (hidden_grad * activated).astype(bf16)
    d_down = lax.psum_scatter(partial, "dp", scatter_dimension=0, tiled=True)
    route_grad = dot_rows(gate_grad, w_gate[0], (1, 1)) + dot_rows(up_grad, w_up[0], (1, 1))
    back = jnp.concatenate([route_grad.astype(bf16), jnp.pad(gate_dots, ((0, 0), (0, 127)))], axis=1)
    arrived = {0: back[REACH * block : (REACH + 1) * block]}
    for d in order:
        arrived[d] = shift(back[(d + REACH) * block : (d + REACH + 1) * block], -d)
    back = jnp.concatenate([arrived[d] for d in range(-REACH, REACH + 1)], axis=0)

    token_part = dot_rows(place, back[:, :width], (0, 0))
    dots = back[:, width].astype(f32).reshape(spread, hubs, cols, CAP).transpose(2, 1, 0, 3)
    dots_tok = jnp.sum(jnp.where(taken_col, dots[:, :, None], 0.0), axis=4)
    dots_route = jnp.sum(jnp.where(named_col, dots_tok[:, :, :, None], 0.0), axis=4)
    dots_route = jnp.pad(dots_route.reshape(cols * hubs * tok, topk), ((0, 0), (0, 128 - topk)))
    home = jnp.concatenate([token_part, dots_route], axis=1).astype(bf16)
    home = lax.all_to_all(home.reshape(cols, hubs * tok, width + 128), "y", 0, 0, tiled=True)
    home = jnp.sum(home.astype(f32), axis=0).reshape(hubs, tok, width + 128)
    from_up = shift(home[1].astype(bf16), -LEAP)
    from_down = shift(home[2].astype(bf16), LEAP)
    total = home[0] + from_up.astype(f32) + from_down.astype(f32)
    d_tokens = total[:, :width].astype(bf16)
    d_gates = total[:, width : width + topk] / gates
    return (d_tokens, d_gates, d_down[None])


def solution(mesh):
    devices = mesh.devices
    dp, node, local = devices.shape
    split = Mesh(devices.reshape(dp, node, local // 2, 2), ("dp", "node", "y", "zh"))
    owner = ("dp", "node", "y", "zh")
    expert = ("node", "y", "zh")
    in_specs = (
        P(owner, None),
        P(owner, None, None),
        P(owner, None),
        P(owner, None),
        P(expert, None, None),
        P(expert, None, None),
        P(expert, None, None),
    )
    out_specs = (P(owner, None), P(owner, None), P(expert, "dp", None))
    return jax.shard_map(shards, mesh=split, in_specs=in_specs, out_specs=out_specs, check_vma=False)
```

```python
import functools

import jax
import jax.numpy as jnp
from jax import lax
from jax.experimental import pallas as pl
from jax.experimental.pallas import tpu as pltpu
from jax.sharding import Mesh, PartitionSpec as P

RING = ("node", "zh")
CAP = 2
COLS = 4
RING_SIZE = 32
SLOTS = COLS * RING_SIZE * CAP
FACTS = 128
VMEM_BYTES = 24 * 1024 * 1024
f32, bf16, i32 = jnp.float32, jnp.bfloat16, jnp.int32


def dot(left, right, contract=(1, 0)):
    dims = ((contract[:1], contract[1:]), ((), ()))
    return lax.dot_general(left, right, dims, preferred_element_type=f32)


def iota(shape, axis):
    return lax.broadcasted_iota(i32, shape, axis)


def expert_of(ring_index, column):
    return (ring_index // 2) * 8 + column * 2 + ring_index % 2


def one_hot(mask):
    return jnp.where(mask, 1.0, 0.0).astype(bf16)


def pack_kernel(routes_ref, gates_ref, grad_ref, pre_ref, out_ref):
    tok, topk = routes_ref.shape
    routes_of, width = tok * topk, pre_ref.shape[1]
    per_col = RING_SIZE * CAP
    routes = routes_ref[...].astype(f32).astype(bf16)
    row_tok, row_k = iota((routes_of, tok), 0) // topk, iota((routes_of, topk), 0) % topk
    spread = dot(one_hot(row_tok == iota((routes_of, tok), 1)), routes)
    named = jnp.sum(jnp.where(row_k == iota((routes_of, topk), 1), spread, 0.0), axis=1, keepdims=True)
    slot = iota((routes_of, SLOTS), 1)
    wanted = expert_of(slot % per_col // CAP, slot // per_col).astype(f32)
    hit = one_hot(named == wanted)
    pair = (routes_of, routes_of)
    earlier = one_hot(iota(pair, 1) // topk < iota(pair, 0) // topk)
    before = dot(earlier, hit)
    pick = jnp.where(before == (slot % CAP).astype(f32), hit.astype(f32), 0.0).astype(bf16)
    rows = dot(pick, pre_ref[...], (0, 0)).astype(bf16)
    gates = gates_ref[...]
    high = gates.astype(bf16)
    rest = gates - high.astype(f32)
    middle = rest.astype(bf16)
    low = (rest - middle.astype(f32)).astype(bf16)
    facts = jnp.zeros((tok, FACTS), f32)
    for at, part in enumerate((routes, high, middle, low)):
        seat = one_hot(iota((topk, FACTS), 1) == iota((topk, FACTS), 0) + at * topk)
        facts = facts + dot(part, seat)
    left = grad_ref.shape[1] - width
    for col in range(COLS):
        out_ref[col, :per_col, :] = rows[col * per_col : (col + 1) * per_col]
        out_ref[col, per_col : per_col + tok, :] = grad_ref[:, :width]
        out_ref[col, per_col + tok :, :left] = grad_ref[:, width:]
        out_ref[col, per_col + tok :, left : left + FACTS] = facts.astype(bf16)
        out_ref[col, per_col + tok :, left + FACTS :] = jnp.zeros((tok, width - left - FACTS), bf16)


def deal_kernel(col_ref, in_ref, out_ref, place_ref, facts_ref, *, tok, topk):
    width = in_ref.shape[2]
    per_col = RING_SIZE * CAP
    left = out_ref.shape[1] - 2 * width
    tokens = COLS * tok
    me = col_ref[0]
    facts = in_ref[:, per_col + tok :, left : left + FACTS].reshape(tokens, FACTS)
    facts_ref[...] = facts
    square = (FACTS, FACTS)
    turned = dot(one_hot(iota(square, 0) == iota(square, 1)), facts, (1, 1))
    gates = turned[topk : 2 * topk] + turned[2 * topk : 3 * topk] + turned[3 * topk : 4 * topk]
    shape = (SLOTS, tokens)
    slot, token = iota(shape, 0), iota(shape, 1)
    wanted = expert_of(slot // (COLS * CAP), me).astype(f32)
    hit = jnp.zeros(shape, f32)
    gate = jnp.zeros(shape, f32)
    for k in range(topk):
        match = turned[k : k + 1] == wanted
        hit = jnp.where(match, 1.0, hit)
        gate = jnp.where(match, gates[k : k + 1], gate)
    pair = (tokens, tokens)
    first, second = iota(pair, 0), iota(pair, 1)
    earlier = jnp.where(first // tok == second // tok, jnp.where(first < second, 1.0, 0.0), 0.0).astype(bf16)
    before = dot(hit.astype(bf16), earlier)
    same = jnp.where(slot % (COLS * CAP) // CAP == token // tok, hit, 0.0)
    place = jnp.where(before == (slot % CAP).astype(f32), same, 0.0)
    scale = jnp.sum(place * gate, axis=1, keepdims=True)
    place = place.astype(bf16)
    eye = one_hot(first == second)
    place_ref[...] = dot(eye, place, (1, 1)).astype(bf16)
    upper = in_ref[:, per_col : per_col + tok, :].reshape(tokens, width)
    lower = in_ref[:, per_col + tok :, :left].reshape(tokens, left)
    out_ref[:, :width] = (dot(place, upper) * scale).astype(bf16)
    out_ref[:, width : width + left] = (dot(place, lower) * scale).astype(bf16)
    square = (SLOTS, SLOTS)
    slot = iota(square, 0)
    origin = slot % (COLS * CAP) // CAP * per_col + slot // (COLS * CAP) * CAP + slot % CAP
    swap = one_hot(origin == iota(square, 1))
    pre = in_ref[:, :per_col, :].reshape(SLOTS, width)
    out_ref[:, width + left :] = dot(swap, pre).astype(bf16)


def join_kernel(col_ref, back_ref, place_ref, facts_ref, out_ref, *, topk):
    tokens = place_ref.shape[0]
    width = out_ref.shape[1] - FACTS
    me = col_ref[0]
    place = place_ref[...]
    out_ref[:, :width] = dot(place, back_ref[:, :width]).astype(bf16)
    lane = (8, FACTS)
    head = one_hot(iota(lane, 1) == iota(lane, 0))
    dots = dot(head, back_ref[:, width:], (1, 1))[0:1]
    held = place.astype(f32) * dots
    shape = (tokens, SLOTS)
    expert = expert_of(iota(shape, 1) // (COLS * CAP), me).astype(f32)
    facts = facts_ref[...].astype(f32)
    lanes = iota((tokens, FACTS), 1)
    result = jnp.zeros((tokens, FACTS), f32)
    for k in range(topk):
        named = jnp.sum(jnp.where(lanes == k, facts, 0.0), axis=1, keepdims=True)
        value = jnp.sum(jnp.where(named == expert, held, 0.0), axis=1, keepdims=True)
        result = jnp.where(lanes == k, value, result)
    out_ref[:, width:] = result.astype(bf16)


def call(kernel, outs, inputs, flops):
    scalar = inputs[0].shape == (1,)
    in_specs = [pl.BlockSpec(memory_space=pltpu.VMEM) for _ in inputs]
    if scalar:
        in_specs[0] = pl.BlockSpec(memory_space=pltpu.SMEM)
    moved = sum(a.size * a.dtype.itemsize for a in inputs) + sum(a.size * a.dtype.itemsize for a in outs)
    return pl.pallas_call(
        kernel,
        out_shape=outs,
        in_specs=in_specs,
        out_specs=[pl.BlockSpec(memory_space=pltpu.VMEM) for _ in outs],
        compiler_params=pltpu.CompilerParams(vmem_limit_bytes=VMEM_BYTES),
        cost_estimate=pl.CostEstimate(flops=flops, bytes_accessed=moved, transcendentals=0),
    )(*inputs)


def shards(grad_out, saved_pre, gates, routes, w_gate, w_up, w_down):
    tok, topk = routes.shape
    width = grad_out.shape[1]
    pre_width = saved_pre.shape[2]
    hidden_width = pre_width // 2
    me_y = lax.axis_index("y").astype(i32).reshape(1)
    out = jax.ShapeDtypeStruct
    per_col = RING_SIZE * CAP
    tokens = COLS * tok

    pre = saved_pre.reshape(tok * topk, pre_width)
    packed = out((COLS, per_col + 2 * tok, pre_width), bf16)
    (packed,) = call(pack_kernel, [packed], (routes, gates, grad_out, pre), 2 * SLOTS * tok * topk * pre_width)
    packed = lax.all_to_all(packed, "y", 0, 0, tiled=True)

    outs = [out((SLOTS, width + pre_width), bf16), out((tokens, SLOTS), bf16), out((tokens, FACTS), bf16)]
    deal = functools.partial(deal_kernel, tok=tok, topk=topk)
    rows, place, facts = call(deal, outs, (me_y, packed), 2 * SLOTS * SLOTS * pre_width)
    rows = rows.reshape(RING_SIZE, COLS * CAP, width + pre_width)
    rows = lax.all_to_all(rows, RING, 0, 0, tiled=True).reshape(SLOTS, width + pre_width)

    weight_rows = rows[:, :width]
    gate_pre = rows[:, width : width + hidden_width].astype(f32)
    up_pre = rows[:, width + hidden_width :].astype(f32)
    sigmoid_gate = jax.nn.sigmoid(gate_pre)
    activated = gate_pre * sigmoid_gate
    hidden = (activated * up_pre).astype(bf16)
    partial = dot(hidden, weight_rows, (0, 0)).astype(bf16)
    hidden_grad = dot(weight_rows, w_down[0], (1, 1))
    gate_dots = jnp.sum(hidden.astype(f32) * hidden_grad, axis=1, keepdims=True).astype(bf16)
    gate_grad = (hidden_grad * up_pre * sigmoid_gate * (1.0 + gate_pre * (1.0 - sigmoid_gate))).astype(bf16)
    up_grad = (hidden_grad * activated).astype(bf16)
    d_down = lax.psum_scatter(partial, "dp", scatter_dimension=0, tiled=True)
    route_grad = dot(gate_grad, w_gate[0], (1, 1)) + dot(up_grad, w_up[0], (1, 1))
    back = jnp.concatenate([route_grad.astype(bf16), jnp.pad(gate_dots, ((0, 0), (0, FACTS - 1)))], axis=1)
    back = lax.all_to_all(back.reshape(RING_SIZE, COLS * CAP, width + FACTS), RING, 0, 0, tiled=True)
    back = back.reshape(SLOTS, width + FACTS)

    join = functools.partial(join_kernel, topk=topk)
    home = [out((tokens, width + FACTS), bf16)]
    (home,) = call(join, home, (me_y, back, place, facts), 2 * tokens * SLOTS * width)
    home = lax.all_to_all(home.reshape(COLS, tok, width + FACTS), "y", 0, 0, tiled=True)
    total = jnp.sum(home.astype(f32), axis=0)
    d_tokens = total[:, :width].astype(bf16)
    d_gates = total[:, width : width + topk] / gates
    return (d_tokens, d_gates, d_down[None])


def solution(mesh):
    devices = mesh.devices
    dp, node, local = devices.shape
    split = Mesh(devices.reshape(dp, node, local // 2, 2), ("dp", "node", "y", "zh"))
    owner = ("dp", "node", "y", "zh")
    expert = ("node", "y", "zh")
    in_specs = (
        P(owner, None),
        P(owner, None, None),
        P(owner, None),
        P(owner, None),
        P(expert, None, None),
        P(expert, None, None),
        P(expert, None, None),
    )
    out_specs = (P(owner, None), P(owner, None), P(expert, "dp", None))
    return jax.shard_map(shards, mesh=split, in_specs=in_specs, out_specs=out_specs, check_vma=False)
```

```python
import functools

import jax
import jax.numpy as jnp
from jax import lax
from jax.experimental import pallas as pl
from jax.experimental.pallas import tpu as pltpu
from jax.sharding import Mesh, PartitionSpec as P

RING = ("zh", "node")
CAP = 2
COLS = 4
RING_SIZE = 32
HALF = RING_SIZE // 2
SLOTS = COLS * RING_SIZE * CAP
FACTS = 128
VMEM_BYTES = 24 * 1024 * 1024
f32, bf16, i32 = jnp.float32, jnp.bfloat16, jnp.int32


def dot(left, right, contract=(1, 0)):
    dims = ((contract[:1], contract[1:]), ((), ()))
    return lax.dot_general(left, right, dims, preferred_element_type=f32)


def iota(shape, axis):
    return lax.broadcasted_iota(i32, shape, axis)


def expert_of(ring_index, column):
    return (ring_index % HALF) * 8 + column * 2 + ring_index // HALF


def one_hot(mask):
    return jnp.where(mask, 1.0, 0.0).astype(bf16)


def pack_kernel(routes_ref, gates_ref, grad_ref, pre_ref, out_ref):
    topk, tok = routes_ref.shape
    routes_of, width = tok * topk, pre_ref.shape[1]
    per_col = RING_SIZE * CAP
    routes = routes_ref[...].astype(f32).astype(bf16)
    row_tok, row_k = iota((routes_of, tok), 0) // topk, iota((routes_of, topk), 0) % topk
    spread = dot(one_hot(row_tok == iota((routes_of, tok), 1)), routes, (1, 1))
    named = jnp.sum(jnp.where(row_k == iota((routes_of, topk), 1), spread, 0.0), axis=1, keepdims=True)
    slot = iota((routes_of, SLOTS), 1)
    wanted = expert_of(slot % per_col // CAP, slot // per_col).astype(f32)
    hit = one_hot(named == wanted)
    pair = (routes_of, routes_of)
    earlier = one_hot(iota(pair, 1) // topk < iota(pair, 0) // topk)
    before = dot(earlier, hit)
    pick = jnp.where(before == (slot % CAP).astype(f32), hit.astype(f32), 0.0).astype(bf16)
    rows = dot(pick, pre_ref[...], (0, 0)).astype(bf16)
    gates = gates_ref[...]
    high = gates.astype(bf16)
    rest = gates - high.astype(f32)
    middle = rest.astype(bf16)
    low = (rest - middle.astype(f32)).astype(bf16)
    facts = jnp.zeros((tok, FACTS), f32)
    for at, part in enumerate((routes, high, middle, low)):
        seat = one_hot(iota((topk, FACTS), 1) == iota((topk, FACTS), 0) + at * topk)
        facts = facts + dot(part, seat, (0, 0))
    left = grad_ref.shape[1] - width
    for col in range(COLS):
        out_ref[col, :per_col, :] = rows[col * per_col : (col + 1) * per_col]
        out_ref[col, per_col : per_col + tok, :] = grad_ref[:, :width]
        out_ref[col, per_col + tok :, :left] = grad_ref[:, width:]
        out_ref[col, per_col + tok :, left : left + FACTS] = facts.astype(bf16)
        out_ref[col, per_col + tok :, left + FACTS :] = jnp.zeros((tok, width - left - FACTS), bf16)


def deal_kernel(col_ref, in_ref, out_ref, place_ref, facts_ref, *, tok, topk):
    width = in_ref.shape[2]
    per_col = RING_SIZE * CAP
    left = out_ref.shape[1] - 2 * width
    tokens = COLS * tok
    me = col_ref[0]
    facts = in_ref[:, per_col + tok :, left : left + FACTS].reshape(tokens, FACTS)
    facts_ref[...] = facts
    square = (FACTS, FACTS)
    turned = dot(one_hot(iota(square, 0) == iota(square, 1)), facts, (1, 1))
    gates = turned[topk : 2 * topk] + turned[2 * topk : 3 * topk] + turned[3 * topk : 4 * topk]
    shape = (SLOTS, tokens)
    slot, token = iota(shape, 0), iota(shape, 1)
    wanted = expert_of(slot // (COLS * CAP), me).astype(f32)
    hit = jnp.zeros(shape, f32)
    gate = jnp.zeros(shape, f32)
    for k in range(topk):
        match = turned[k : k + 1] == wanted
        hit = jnp.where(match, 1.0, hit)
        gate = jnp.where(match, gates[k : k + 1], gate)
    pair = (tokens, tokens)
    first, second = iota(pair, 0), iota(pair, 1)
    earlier = jnp.where(first // tok == second // tok, jnp.where(first < second, 1.0, 0.0), 0.0).astype(bf16)
    before = dot(hit.astype(bf16), earlier)
    same = jnp.where(slot % (COLS * CAP) // CAP == token // tok, hit, 0.0)
    place = jnp.where(before == (slot % CAP).astype(f32), same, 0.0)
    scale = jnp.sum(place * gate, axis=1, keepdims=True)
    place = place.astype(bf16)
    eye = one_hot(first == second)
    place_ref[...] = dot(eye, place, (1, 1)).astype(bf16)
    upper = in_ref[:, per_col : per_col + tok, :].reshape(tokens, width)
    lower = in_ref[:, per_col + tok :, :left].reshape(tokens, left)
    out_ref[:, :width] = (dot(place, upper) * scale).astype(bf16)
    out_ref[:, width : width + left] = (dot(place, lower) * scale).astype(bf16)
    square = (SLOTS, SLOTS)
    slot = iota(square, 0)
    origin = slot % (COLS * CAP) // CAP * per_col + slot // (COLS * CAP) * CAP + slot % CAP
    swap = one_hot(origin == iota(square, 1))
    pre = in_ref[:, :per_col, :].reshape(SLOTS, width)
    out_ref[:, width + left :] = dot(swap, pre).astype(bf16)


def join_kernel(col_ref, back_ref, place_ref, facts_ref, out_ref, *, topk):
    tokens = place_ref.shape[0]
    width = out_ref.shape[1] - FACTS
    me = col_ref[0]
    place = place_ref[...]
    out_ref[:, :width] = dot(place, back_ref[:, :width]).astype(bf16)
    lane = (8, FACTS)
    head = one_hot(iota(lane, 1) == iota(lane, 0))
    dots = dot(head, back_ref[:, width:], (1, 1))[0:1]
    held = place.astype(f32) * dots
    shape = (tokens, SLOTS)
    expert = expert_of(iota(shape, 1) // (COLS * CAP), me).astype(f32)
    facts = facts_ref[...].astype(f32)
    lanes = iota((tokens, FACTS), 1)
    result = jnp.zeros((tokens, FACTS), f32)
    for k in range(topk):
        named = jnp.sum(jnp.where(lanes == k, facts, 0.0), axis=1, keepdims=True)
        value = jnp.sum(jnp.where(named == expert, held, 0.0), axis=1, keepdims=True)
        result = jnp.where(lanes == k, value, result)
    out_ref[:, width:] = result.astype(bf16)


def call(kernel, outs, inputs, flops):
    scalar = inputs[0].shape == (1,)
    in_specs = [pl.BlockSpec(memory_space=pltpu.VMEM) for _ in inputs]
    if scalar:
        in_specs[0] = pl.BlockSpec(memory_space=pltpu.SMEM)
    moved = sum(a.size * a.dtype.itemsize for a in inputs) + sum(a.size * a.dtype.itemsize for a in outs)
    return pl.pallas_call(
        kernel,
        out_shape=outs,
        in_specs=in_specs,
        out_specs=[pl.BlockSpec(memory_space=pltpu.VMEM) for _ in outs],
        compiler_params=pltpu.CompilerParams(vmem_limit_bytes=VMEM_BYTES),
        cost_estimate=pl.CostEstimate(flops=flops, bytes_accessed=moved, transcendentals=0),
    )(*inputs)


def shards(grad_out, saved_pre, gates, routes, w_gate, w_up, w_down):
    tok, topk = routes.shape
    width = grad_out.shape[1]
    pre_width = saved_pre.shape[2]
    hidden_width = pre_width // 2
    me_y = lax.axis_index("y").astype(i32).reshape(1)
    out = jax.ShapeDtypeStruct
    per_col = RING_SIZE * CAP
    tokens = COLS * tok

    pre = saved_pre.reshape(tok * topk, pre_width)
    packed = out((COLS, per_col + 2 * tok, pre_width), bf16)
    (packed,) = call(pack_kernel, [packed], (routes.T, gates.T, grad_out, pre), 2 * SLOTS * tok * topk * pre_width)
    packed = lax.all_to_all(packed, "y", 0, 0, tiled=True)

    outs = [out((SLOTS, width + pre_width), bf16), out((tokens, SLOTS), bf16), out((tokens, FACTS), bf16)]
    deal = functools.partial(deal_kernel, tok=tok, topk=topk)
    rows, place, facts = call(deal, outs, (me_y, packed), 2 * SLOTS * SLOTS * pre_width)
    rows = rows.reshape(RING_SIZE, COLS * CAP, width + pre_width)
    rows = lax.all_to_all(rows, RING, 0, 0, tiled=True).reshape(SLOTS, width + pre_width)

    weight_rows = rows[:, :width]
    gate_pre = rows[:, width : width + hidden_width].astype(f32)
    up_pre = rows[:, width + hidden_width :].astype(f32)
    sigmoid_gate = jax.nn.sigmoid(gate_pre)
    activated = gate_pre * sigmoid_gate
    hidden = (activated * up_pre).astype(bf16)
    partial = dot(hidden, weight_rows, (0, 0)).astype(bf16)
    hidden_grad = dot(weight_rows, w_down[0], (1, 1))
    gate_dots = jnp.sum(hidden.astype(f32) * hidden_grad, axis=1, keepdims=True).astype(bf16)
    gate_grad = (hidden_grad * up_pre * sigmoid_gate * (1.0 + gate_pre * (1.0 - sigmoid_gate))).astype(bf16)
    up_grad = (hidden_grad * activated).astype(bf16)
    d_down = lax.psum_scatter(partial, "dp", scatter_dimension=0, tiled=True)
    route_grad = dot(gate_grad, w_gate[0], (1, 1)) + dot(up_grad, w_up[0], (1, 1))
    back = jnp.concatenate([route_grad.astype(bf16), jnp.pad(gate_dots, ((0, 0), (0, FACTS - 1)))], axis=1)
    back = lax.all_to_all(back.reshape(RING_SIZE, COLS * CAP, width + FACTS), RING, 0, 0, tiled=True)
    back = back.reshape(SLOTS, width + FACTS)

    join = functools.partial(join_kernel, topk=topk)
    home = [out((tokens, width + FACTS), bf16)]
    (home,) = call(join, home, (me_y, back, place, facts), 2 * tokens * SLOTS * width)
    home = lax.all_to_all(home.reshape(COLS, tok, width + FACTS), "y", 0, 0, tiled=True)
    total = jnp.sum(home.astype(f32), axis=0)
    d_tokens = total[:, :width].astype(bf16)
    d_gates = total[:, width : width + topk] / gates
    return (d_tokens, d_gates, d_down[None])


def solution(mesh):
    devices = mesh.devices
    dp, node, local = devices.shape
    split = Mesh(devices.reshape(dp, node, local // 2, 2), ("dp", "node", "y", "zh"))
    owner = ("dp", "node", "y", "zh")
    expert = ("node", "y", "zh")
    in_specs = (
        P(owner, None),
        P(owner, None, None),
        P(owner, None),
        P(owner, None),
        P(expert, None, None),
        P(expert, None, None),
        P(expert, None, None),
    )
    out_specs = (P(owner, None), P(owner, None), P(expert, "dp", None))
    return jax.shard_map(shards, mesh=split, in_specs=in_specs, out_specs=out_specs, check_vma=False)
```

```python
import functools

import jax
import jax.numpy as jnp
from jax import lax
from jax.experimental import pallas as pl
from jax.experimental.pallas import tpu as pltpu
from jax.sharding import Mesh, PartitionSpec as P

RING = ("zh", "node")
CAP = 2
COLS = 4
RING_SIZE = 32
HALF = RING_SIZE // 2
SLOTS = COLS * RING_SIZE * CAP
FACTS = 128
RAISES = (64, 32, 8, 4, 2, 1)
MIDDLE = 2.0**14
LOW = 2.0**20
VMEM_BYTES = 24 * 1024 * 1024
f32, bf16, i32 = jnp.float32, jnp.bfloat16, jnp.int32


def dot(left, right, contract=(1, 0)):
    dims = ((contract[:1], contract[1:]), ((), ()))
    return lax.dot_general(left, right, dims, preferred_element_type=f32)


def iota(shape, axis):
    return lax.broadcasted_iota(i32, shape, axis)


def expert_of(ring_index, column):
    return (ring_index % HALF) * 8 + column * 2 + ring_index // HALF


def one_hot(mask):
    return jnp.where(mask, 1.0, 0.0).astype(bf16)


def pack_kernel(routes_ref, gates_ref, grad_ref, pre_ref, out_ref, tokens_ref):
    topk, tok = routes_ref.shape
    routes_of, width = tok * topk, pre_ref.shape[1]
    per_col = RING_SIZE * CAP
    routes = routes_ref[...].astype(f32).astype(bf16)
    row_tok, row_k = iota((routes_of, tok), 0) // topk, iota((routes_of, topk), 0) % topk
    spread = dot(one_hot(row_tok == iota((routes_of, tok), 1)), routes, (1, 1))
    named = jnp.sum(jnp.where(row_k == iota((routes_of, topk), 1), spread, 0.0), axis=1, keepdims=True)
    slot = iota((routes_of, SLOTS), 1)
    wanted = expert_of(slot % per_col // CAP, slot // per_col).astype(f32)
    hit = one_hot(named == wanted)
    pair = (routes_of, routes_of)
    earlier = one_hot(iota(pair, 1) // topk < iota(pair, 0) // topk)
    before = dot(earlier, hit)
    pick = jnp.where(before == (slot % CAP).astype(f32), hit.astype(f32), 0.0).astype(bf16)
    rows = dot(pick, pre_ref[...], (0, 0)).astype(bf16)
    gates = gates_ref[...]
    high = gates.astype(bf16)
    rest = gates - high.astype(f32)
    middle = rest.astype(bf16)
    low = (rest - middle.astype(f32)).astype(bf16)
    seats = [one_hot(iota((topk, FACTS), 1) == iota((topk, FACTS), 0) + at * topk) for at in range(4)]
    named = dot(routes, seats[0], (0, 0))
    facts = named + dot(high, seats[1], (0, 0)) + dot(middle, seats[2], (0, 0)) * MIDDLE
    facts = facts + dot(low, seats[3], (0, 0)) * LOW
    grad = grad_ref[...].astype(f32)
    top = jnp.max(jnp.abs(grad), axis=1, keepdims=True)
    scale, raised = jnp.ones((tok, 1), f32), jnp.zeros((tok, 1), f32)
    for step in RAISES:
        fits = top * (scale * 2.0**step) <= 2.0**15
        scale = jnp.where(fits, scale * 2.0**step, scale)
        raised = jnp.where(fits, raised + step, raised)
    facts = jnp.where(iota((tok, FACTS), 1) == 4 * topk, raised, facts)
    tokens_ref[:, : grad.shape[1]] = grad * scale
    tokens_ref[:, grad.shape[1] :] = facts
    for col in range(COLS):
        out_ref[col, :per_col, :] = rows[col * per_col : (col + 1) * per_col]
        out_ref[col, per_col:, :FACTS] = named.astype(bf16)
        out_ref[col, per_col:, FACTS:] = jnp.zeros((tok, width - FACTS), bf16)


def deal_kernel(col_ref, in_ref, out_ref, place_ref, facts_ref, *, tok, topk):
    width = in_ref.shape[2]
    per_col = RING_SIZE * CAP
    tokens = COLS * tok
    me = col_ref[0]
    facts = in_ref[:, per_col:, :FACTS].reshape(tokens, FACTS)
    facts_ref[...] = facts
    square = (FACTS, FACTS)
    turned = dot(one_hot(iota(square, 0) == iota(square, 1)), facts, (1, 1))
    shape = (SLOTS, tokens)
    slot, token = iota(shape, 0), iota(shape, 1)
    wanted = expert_of(slot // (COLS * CAP), me).astype(f32)
    hit = jnp.zeros(shape, f32)
    for k in range(topk):
        hit = jnp.where(turned[k : k + 1] == wanted, 1.0, hit)
    pair = (tokens, tokens)
    first, second = iota(pair, 0), iota(pair, 1)
    earlier = jnp.where(first // tok == second // tok, jnp.where(first < second, 1.0, 0.0), 0.0).astype(bf16)
    before = dot(hit.astype(bf16), earlier)
    same = jnp.where(slot % (COLS * CAP) // CAP == token // tok, hit, 0.0)
    place = jnp.where(before == (slot % CAP).astype(f32), same, 0.0).astype(bf16)
    eye = one_hot(first == second)
    place_ref[...] = dot(eye, place, (1, 1)).astype(bf16)
    square = (SLOTS, SLOTS)
    slot = iota(square, 0)
    origin = slot % (COLS * CAP) // CAP * per_col + slot // (COLS * CAP) * CAP + slot % CAP
    swap = one_hot(origin == iota(square, 1))
    out_ref[...] = dot(swap, in_ref[:, :per_col, :].reshape(SLOTS, width)).astype(bf16)


def weigh_kernel(at_ref, in_ref, *out_refs, tok, topk):
    tokens = in_ref.shape[0]
    width = in_ref.shape[1] - FACTS
    me, place_me = at_ref[0], at_ref[1]
    square = (FACTS, FACTS)
    turned = dot(one_hot(iota(square, 0) == iota(square, 1)), in_ref[:, width:], (1, 1))
    routes = turned[:topk]
    gates = turned[topk : 2 * topk] + turned[2 * topk : 3 * topk] * (1.0 / MIDDLE)
    gates = gates + turned[3 * topk : 4 * topk] * (1.0 / LOW)
    raised = turned[4 * topk : 4 * topk + 1]
    lower = jnp.ones((1, tokens), f32)
    for step in RAISES:
        has = raised >= step
        lower = jnp.where(has, lower * 2.0**-step, lower)
        raised = jnp.where(has, raised - step, raised)
    hits, gate = [], []
    stack = jnp.zeros((8, tokens), f32)
    row = iota((8, tokens), 0)
    for col in range(COLS):
        wanted = expert_of(place_me, (me + col) % COLS).astype(f32)
        match = routes == wanted
        hits.append(jnp.sum(jnp.where(match, 1.0, 0.0), axis=0, keepdims=True))
        gate.append(jnp.sum(jnp.where(match, gates, 0.0), axis=0, keepdims=True))
        stack = jnp.where(row == col, hits[col], stack)
    pair = (tokens, tokens)
    first, second = iota(pair, 0), iota(pair, 1)
    earlier = jnp.where(first // tok == second // tok, jnp.where(first < second, 1.0, 0.0), 0.0).astype(bf16)
    before = dot(stack.astype(bf16), earlier)
    shape = (RING_SIZE * CAP, tokens)
    slot, token = iota(shape, 0), iota(shape, 1)
    for col in range(COLS):
        place = jnp.where(slot // CAP == token // tok, hits[col], 0.0)
        place = jnp.where(before[col : col + 1] == (slot % CAP).astype(f32), place, 0.0)
        scale = jnp.sum(place * gate[col], axis=1, keepdims=True)
        unit = jnp.sum(place * lower, axis=1, keepdims=True)
        rows = dot(place.astype(bf16), in_ref[:, :width]) * unit
        out_refs[col][...] = (rows * scale).astype(bf16)


def gather_kernel(col_ref, *refs):
    in_refs, out_ref = refs[:-1], refs[-1]
    me = col_ref[0]
    per_col = RING_SIZE * CAP
    shape = (SLOTS, per_col)
    slot = iota(shape, 0)
    column = slot % (COLS * CAP) // CAP
    origin = slot // (COLS * CAP) * CAP + slot % CAP
    total = jnp.zeros(out_ref.shape, f32)
    for hop, ref in enumerate(in_refs):
        away = (me - hop + COLS) % COLS
        picked = jnp.where(column == away, jnp.where(origin == iota(shape, 1), 1.0, 0.0), 0.0)
        total = total + dot(picked.astype(bf16), ref[...])
    out_ref[...] = total.astype(bf16)


def join_kernel(col_ref, back_ref, place_ref, facts_ref, out_ref, *, topk):
    tokens = place_ref.shape[0]
    width = out_ref.shape[1] - FACTS
    me = col_ref[0]
    place = place_ref[...]
    out_ref[:, :width] = dot(place, back_ref[:, :width]).astype(bf16)
    lane = (8, FACTS)
    head = one_hot(iota(lane, 1) == iota(lane, 0))
    dots = dot(head, back_ref[:, width:], (1, 1))[0:1]
    held = place.astype(f32) * dots
    shape = (tokens, SLOTS)
    expert = expert_of(iota(shape, 1) // (COLS * CAP), me).astype(f32)
    facts = facts_ref[...].astype(f32)
    lanes = iota((tokens, FACTS), 1)
    result = jnp.zeros((tokens, FACTS), f32)
    for k in range(topk):
        named = jnp.sum(jnp.where(lanes == k, facts, 0.0), axis=1, keepdims=True)
        value = jnp.sum(jnp.where(named == expert, held, 0.0), axis=1, keepdims=True)
        result = jnp.where(lanes == k, value, result)
    out_ref[:, width:] = result.astype(bf16)


def call(kernel, outs, inputs, flops):
    scalar = inputs[0].ndim == 1
    in_specs = [pl.BlockSpec(memory_space=pltpu.VMEM) for _ in inputs]
    if scalar:
        in_specs[0] = pl.BlockSpec(memory_space=pltpu.SMEM)
    moved = sum(a.size * a.dtype.itemsize for a in inputs) + sum(a.size * a.dtype.itemsize for a in outs)
    return pl.pallas_call(
        kernel,
        out_shape=outs,
        in_specs=in_specs,
        out_specs=[pl.BlockSpec(memory_space=pltpu.VMEM) for _ in outs],
        compiler_params=pltpu.CompilerParams(vmem_limit_bytes=VMEM_BYTES),
        cost_estimate=pl.CostEstimate(flops=flops, bytes_accessed=moved, transcendentals=0),
    )(*inputs)


def shards(grad_out, saved_pre, gates, routes, w_gate, w_up, w_down):
    tok, topk = routes.shape
    width = grad_out.shape[1]
    pre_width = saved_pre.shape[2]
    hidden_width = pre_width // 2
    me_y = lax.axis_index("y").astype(i32).reshape(1)
    me_z = (lax.axis_index("zh") * HALF + lax.axis_index("node")).astype(i32).reshape(1)
    out = jax.ShapeDtypeStruct
    per_col = RING_SIZE * CAP
    tokens = COLS * tok

    pre = saved_pre.reshape(tok * topk, pre_width)
    outs = [out((COLS, per_col + tok, pre_width), bf16), out((tok, width + FACTS), f32)]
    inputs = (routes.T, gates.T, grad_out, pre)
    packed, own = call(pack_kernel, outs, inputs, 2 * SLOTS * tok * topk * pre_width)
    packed = lax.all_to_all(packed, "y", 0, 0, tiled=True)

    ring_tokens = lax.all_gather(own.astype(jnp.float16), RING, axis=0, tiled=True)
    outs = [out((SLOTS, pre_width), bf16), out((tokens, SLOTS), bf16), out((tokens, FACTS), bf16)]
    deal = functools.partial(deal_kernel, tok=tok, topk=topk)
    pre_rows, place, facts = call(deal, outs, (me_y, packed), 2 * SLOTS * SLOTS * pre_width)
    pre_rows, ring_tokens = lax.optimization_barrier((pre_rows, ring_tokens))
    pre_rows = lax.all_to_all(pre_rows.reshape(RING_SIZE, COLS * CAP, pre_width), RING, 0, 0, tiled=True)
    pre_rows = pre_rows.reshape(SLOTS, pre_width)

    weigh = functools.partial(weigh_kernel, tok=tok, topk=topk)
    outs = [out((per_col, width), bf16)] * COLS
    at = jnp.concatenate([me_y, me_z])
    sent = call(weigh, outs, (at, ring_tokens.astype(bf16)), 2 * SLOTS * tok * RING_SIZE * width)
    came = [sent[0]]
    for hop in range(1, COLS):
        came.append(lax.ppermute(sent[hop], "y", [(col, (col + hop) % COLS) for col in range(COLS)]))
    outs = [out((SLOTS, width), bf16)]
    (weight_rows,) = call(gather_kernel, outs, (me_y, *came), 2 * SLOTS * SLOTS * width)

    gate_pre = pre_rows[:, :hidden_width].astype(f32)
    up_pre = pre_rows[:, hidden_width:].astype(f32)
    sigmoid_gate = jax.nn.sigmoid(gate_pre)
    activated = gate_pre * sigmoid_gate
    hidden = (activated * up_pre).astype(bf16)
    partial = dot(hidden, weight_rows, (0, 0)).astype(bf16)
    hidden_grad = dot(weight_rows, w_down[0], (1, 1))
    gate_dots = jnp.sum(hidden.astype(f32) * hidden_grad, axis=1, keepdims=True).astype(bf16)
    gate_grad = (hidden_grad * up_pre * sigmoid_gate * (1.0 + gate_pre * (1.0 - sigmoid_gate))).astype(bf16)
    up_grad = (hidden_grad * activated).astype(bf16)
    d_down = lax.psum_scatter(partial, "dp", scatter_dimension=0, tiled=True)
    route_grad = dot(gate_grad, w_gate[0], (1, 1)) + dot(up_grad, w_up[0], (1, 1))
    back = jnp.concatenate([route_grad.astype(bf16), jnp.pad(gate_dots, ((0, 0), (0, FACTS - 1)))], axis=1)
    back = lax.all_to_all(back.reshape(RING_SIZE, COLS * CAP, width + FACTS), RING, 0, 0, tiled=True)
    back = back.reshape(SLOTS, width + FACTS)

    join = functools.partial(join_kernel, topk=topk)
    home = [out((tokens, width + FACTS), bf16)]
    (home,) = call(join, home, (me_y, back, place, facts), 2 * tokens * SLOTS * width)
    home = lax.all_to_all(home.reshape(COLS, tok, width + FACTS), "y", 0, 0, tiled=True)
    total = jnp.sum(home.astype(f32), axis=0)
    d_tokens = total[:, :width].astype(bf16)
    d_gates = total[:, width : width + topk] / gates
    return (d_tokens, d_gates, d_down[None])


def solution(mesh):
    devices = mesh.devices
    dp, node, local = devices.shape
    split = Mesh(devices.reshape(dp, node, local // 2, 2), ("dp", "node", "y", "zh"))
    owner = ("dp", "node", "y", "zh")
    expert = ("node", "y", "zh")
    in_specs = (
        P(owner, None),
        P(owner, None, None),
        P(owner, None),
        P(owner, None),
        P(expert, None, None),
        P(expert, None, None),
        P(expert, None, None),
    )
    out_specs = (P(owner, None), P(owner, None), P(expert, "dp", None))
    return jax.shard_map(shards, mesh=split, in_specs=in_specs, out_specs=out_specs, check_vma=False)
```

```python
import functools

import jax
import jax.numpy as jnp
from jax import lax
from jax.experimental import pallas as pl
from jax.experimental.pallas import tpu as pltpu
from jax.sharding import Mesh, PartitionSpec as P

RING = ("zh", "node")
CAP = 2
COLS = 4
RING_SIZE = 32
HALF = RING_SIZE // 2
SLOTS = COLS * RING_SIZE * CAP
FACTS = 128
RAISES = (64, 32, 8, 4, 2, 1)
MIDDLE = 2.0**14
LOW = 2.0**20
VMEM_BYTES = 24 * 1024 * 1024
f32, bf16, i32 = jnp.float32, jnp.bfloat16, jnp.int32


def dot(left, right, contract=(1, 0)):
    dims = ((contract[:1], contract[1:]), ((), ()))
    return lax.dot_general(left, right, dims, preferred_element_type=f32)


def iota(shape, axis):
    return lax.broadcasted_iota(i32, shape, axis)


def expert_of(ring_index, column):
    return (ring_index % HALF) * 8 + column * 2 + ring_index // HALF


def one_hot(mask):
    return jnp.where(mask, 1.0, 0.0).astype(bf16)


def pack_kernel(routes_ref, gates_ref, grad_ref, pre_ref, out_ref, tokens_ref):
    topk, tok = routes_ref.shape
    routes_of, width = tok * topk, pre_ref.shape[1]
    per_col = RING_SIZE * CAP
    routes = routes_ref[...].astype(f32).astype(bf16)
    row_tok, row_k = iota((routes_of, tok), 0) // topk, iota((routes_of, topk), 0) % topk
    spread = dot(one_hot(row_tok == iota((routes_of, tok), 1)), routes, (1, 1))
    named = jnp.sum(jnp.where(row_k == iota((routes_of, topk), 1), spread, 0.0), axis=1, keepdims=True)
    slot = iota((routes_of, SLOTS), 1)
    wanted = expert_of(slot % per_col // CAP, slot // per_col).astype(f32)
    hit = one_hot(named == wanted)
    pair = (routes_of, routes_of)
    earlier = one_hot(iota(pair, 1) // topk < iota(pair, 0) // topk)
    before = dot(earlier, hit)
    pick = jnp.where(before == (slot % CAP).astype(f32), hit.astype(f32), 0.0).astype(bf16)
    rows = dot(pick, pre_ref[...], (0, 0)).astype(bf16)
    gates = gates_ref[...]
    high = gates.astype(bf16)
    rest = gates - high.astype(f32)
    middle = rest.astype(bf16)
    low = (rest - middle.astype(f32)).astype(bf16)
    seats = [one_hot(iota((topk, FACTS), 1) == iota((topk, FACTS), 0) + at * topk) for at in range(4)]
    named = dot(routes, seats[0], (0, 0))
    facts = named + dot(high, seats[1], (0, 0)) + dot(middle, seats[2], (0, 0)) * MIDDLE
    facts = facts + dot(low, seats[3], (0, 0)) * LOW
    grad = grad_ref[...].astype(f32)
    top = jnp.max(jnp.abs(grad), axis=1, keepdims=True)
    scale, raised = jnp.ones((tok, 1), f32), jnp.zeros((tok, 1), f32)
    for step in RAISES:
        fits = top * (scale * 2.0**step) <= 2.0**15
        scale = jnp.where(fits, scale * 2.0**step, scale)
        raised = jnp.where(fits, raised + step, raised)
    facts = jnp.where(iota((tok, FACTS), 1) == 4 * topk, raised, facts)
    tokens_ref[:, : grad.shape[1]] = grad * scale
    tokens_ref[:, grad.shape[1] :] = facts
    for col in range(COLS):
        out_ref[col, :per_col, :] = rows[col * per_col : (col + 1) * per_col]
        out_ref[col, per_col:, :FACTS] = named.astype(bf16)
        out_ref[col, per_col:, FACTS:] = jnp.zeros((tok, width - FACTS), bf16)


def deal_kernel(col_ref, in_ref, out_ref, place_ref, facts_ref, *, tok, topk):
    width = in_ref.shape[2]
    per_col = RING_SIZE * CAP
    tokens = COLS * tok
    me = col_ref[0]
    facts = in_ref[:, per_col:, :FACTS].reshape(tokens, FACTS)
    facts_ref[...] = facts
    square = (FACTS, FACTS)
    turned = dot(one_hot(iota(square, 0) == iota(square, 1)), facts, (1, 1))
    shape = (SLOTS, tokens)
    slot, token = iota(shape, 0), iota(shape, 1)
    wanted = expert_of(slot // (COLS * CAP), me).astype(f32)
    hit = jnp.zeros(shape, f32)
    for k in range(topk):
        hit = jnp.where(turned[k : k + 1] == wanted, 1.0, hit)
    pair = (tokens, tokens)
    first, second = iota(pair, 0), iota(pair, 1)
    earlier = jnp.where(first // tok == second // tok, jnp.where(first < second, 1.0, 0.0), 0.0).astype(bf16)
    before = dot(hit.astype(bf16), earlier)
    same = jnp.where(slot % (COLS * CAP) // CAP == token // tok, hit, 0.0)
    place = jnp.where(before == (slot % CAP).astype(f32), same, 0.0).astype(bf16)
    eye = one_hot(first == second)
    place_ref[...] = dot(eye, place, (1, 1)).astype(bf16)
    square = (SLOTS, SLOTS)
    slot = iota(square, 0)
    origin = slot % (COLS * CAP) // CAP * per_col + slot // (COLS * CAP) * CAP + slot % CAP
    swap = one_hot(origin == iota(square, 1))
    out_ref[...] = dot(swap, in_ref[:, :per_col, :].reshape(SLOTS, width)).astype(bf16)


def weigh_kernel(at_ref, in_ref, *out_refs, tok, topk):
    tokens = in_ref.shape[0]
    width = in_ref.shape[1] - FACTS
    me, place_me = at_ref[0], at_ref[1]
    square = (FACTS, FACTS)
    turned = dot(one_hot(iota(square, 0) == iota(square, 1)), in_ref[:, width:], (1, 1))
    routes = turned[:topk]
    gates = turned[topk : 2 * topk] + turned[2 * topk : 3 * topk] * (1.0 / MIDDLE)
    gates = gates + turned[3 * topk : 4 * topk] * (1.0 / LOW)
    raised = turned[4 * topk : 4 * topk + 1]
    lower = jnp.ones((1, tokens), f32)
    for step in RAISES:
        has = raised >= step
        lower = jnp.where(has, lower * 2.0**-step, lower)
        raised = jnp.where(has, raised - step, raised)
    hits, gate = [], []
    stack = jnp.zeros((8, tokens), f32)
    row = iota((8, tokens), 0)
    for col in range(COLS):
        wanted = expert_of(place_me, (me + col) % COLS).astype(f32)
        match = routes == wanted
        hits.append(jnp.sum(jnp.where(match, 1.0, 0.0), axis=0, keepdims=True))
        gate.append(jnp.sum(jnp.where(match, gates, 0.0), axis=0, keepdims=True))
        stack = jnp.where(row == col, hits[col], stack)
    pair = (tokens, tokens)
    first, second = iota(pair, 0), iota(pair, 1)
    earlier = jnp.where(first // tok == second // tok, jnp.where(first < second, 1.0, 0.0), 0.0).astype(bf16)
    before = dot(stack.astype(bf16), earlier)
    shape = (RING_SIZE * CAP, tokens)
    slot, token = iota(shape, 0), iota(shape, 1)
    for col in range(COLS):
        place = jnp.where(slot // CAP == token // tok, hits[col], 0.0)
        place = jnp.where(before[col : col + 1] == (slot % CAP).astype(f32), place, 0.0)
        scale = jnp.sum(place * gate[col], axis=1, keepdims=True)
        unit = jnp.sum(place * lower, axis=1, keepdims=True)
        rows = dot(place.astype(bf16), in_ref[:, :width]) * unit
        out_refs[col][...] = (rows * scale).astype(bf16)


def gather_kernel(col_ref, *refs):
    in_refs, out_ref = refs[:-1], refs[-1]
    me = col_ref[0]
    per_col = RING_SIZE * CAP
    shape = (SLOTS, per_col)
    slot = iota(shape, 0)
    column = slot % (COLS * CAP) // CAP
    origin = slot // (COLS * CAP) * CAP + slot % CAP
    total = jnp.zeros(out_ref.shape, f32)
    for hop, ref in enumerate(in_refs):
        away = (me - hop + COLS) % COLS
        picked = jnp.where(column == away, jnp.where(origin == iota(shape, 1), 1.0, 0.0), 0.0)
        total = total + dot(picked.astype(bf16), ref[...])
    out_ref[...] = total.astype(bf16)


def join_kernel(col_ref, back_ref, place_ref, facts_ref, out_ref, *, topk):
    tokens = place_ref.shape[0]
    width = out_ref.shape[1] - FACTS
    me = col_ref[0]
    place = place_ref[...]
    out_ref[:, :width] = dot(place, back_ref[:, :width]).astype(bf16)
    lane = (8, FACTS)
    head = one_hot(iota(lane, 1) == iota(lane, 0))
    dots = dot(head, back_ref[:, width:], (1, 1))[0:1]
    held = place.astype(f32) * dots
    shape = (tokens, SLOTS)
    expert = expert_of(iota(shape, 1) // (COLS * CAP), me).astype(f32)
    facts = facts_ref[...].astype(f32)
    lanes = iota((tokens, FACTS), 1)
    result = jnp.zeros((tokens, FACTS), f32)
    for k in range(topk):
        named = jnp.sum(jnp.where(lanes == k, facts, 0.0), axis=1, keepdims=True)
        value = jnp.sum(jnp.where(named == expert, held, 0.0), axis=1, keepdims=True)
        result = jnp.where(lanes == k, value, result)
    out_ref[:, width:] = result.astype(bf16)


def expert_kernel(rows_ref, pre_ref, gate_ref, up_ref, down_ref, back_ref, hidden_ref):
    hidden_width = down_ref.shape[0]
    width = down_ref.shape[1]
    gate_pre = pre_ref[:, :hidden_width].astype(f32)
    up_pre = pre_ref[:, hidden_width:].astype(f32)
    sigmoid_gate = jax.nn.sigmoid(gate_pre)
    activated = gate_pre * sigmoid_gate
    hidden = (activated * up_pre).astype(bf16)
    hidden_ref[...] = hidden
    hidden_grad = dot(rows_ref[...], down_ref[...], (1, 1))
    dots = jnp.sum(hidden.astype(f32) * hidden_grad, axis=1, keepdims=True)
    lanes = iota((rows_ref.shape[0], FACTS), 1)
    back_ref[:, width:] = jnp.where(lanes == 0, dots, 0.0).astype(bf16)
    gate_grad = (hidden_grad * up_pre * sigmoid_gate * (1.0 + gate_pre * (1.0 - sigmoid_gate))).astype(bf16)
    up_grad = (hidden_grad * activated).astype(bf16)
    route_grad = dot(gate_grad, gate_ref[...], (1, 1)) + dot(up_grad, up_ref[...], (1, 1))
    back_ref[:, :width] = route_grad.astype(bf16)


def finish_kernel(home_ref, gates_ref, tokens_ref, gates_out_ref):
    width = tokens_ref.shape[1]
    topk = gates_ref.shape[0]
    total = home_ref[0].astype(f32)
    for col in range(1, COLS):
        total = total + home_ref[col].astype(f32)
    tokens_ref[...] = total[:, :width].astype(bf16)
    seat = one_hot(iota((topk, FACTS), 1) == iota((topk, FACTS), 0))
    gates_out_ref[...] = dot(seat, total[:, width:].astype(bf16), (1, 1)) / gates_ref[...]


def call(kernel, outs, inputs, flops):
    scalar = inputs[0].ndim == 1
    in_specs = [pl.BlockSpec(memory_space=pltpu.VMEM) for _ in inputs]
    if scalar:
        in_specs[0] = pl.BlockSpec(memory_space=pltpu.SMEM)
    moved = sum(a.size * a.dtype.itemsize for a in inputs) + sum(a.size * a.dtype.itemsize for a in outs)
    return pl.pallas_call(
        kernel,
        out_shape=outs,
        in_specs=in_specs,
        out_specs=[pl.BlockSpec(memory_space=pltpu.VMEM) for _ in outs],
        compiler_params=pltpu.CompilerParams(vmem_limit_bytes=VMEM_BYTES),
        cost_estimate=pl.CostEstimate(flops=flops, bytes_accessed=moved, transcendentals=0),
    )(*inputs)


def shards(grad_out, saved_pre, gates, routes, w_gate, w_up, w_down):
    tok, topk = routes.shape
    width = grad_out.shape[1]
    pre_width = saved_pre.shape[2]
    hidden_width = pre_width // 2
    me_y = lax.axis_index("y").astype(i32).reshape(1)
    me_z = (lax.axis_index("zh") * HALF + lax.axis_index("node")).astype(i32).reshape(1)
    out = jax.ShapeDtypeStruct
    per_col = RING_SIZE * CAP
    tokens = COLS * tok

    pre = saved_pre.reshape(tok * topk, pre_width)
    outs = [out((COLS, per_col + tok, pre_width), bf16), out((tok, width + FACTS), f32)]
    inputs = (routes.T, gates.T, grad_out, pre)
    packed, own = call(pack_kernel, outs, inputs, 2 * SLOTS * tok * topk * pre_width)
    packed = lax.all_to_all(packed, "y", 0, 0, tiled=True)

    ring_tokens = lax.all_gather(own.astype(jnp.float16), RING, axis=0, tiled=True)
    outs = [out((SLOTS, pre_width), bf16), out((tokens, SLOTS), bf16), out((tokens, FACTS), bf16)]
    deal = functools.partial(deal_kernel, tok=tok, topk=topk)
    pre_rows, place, facts = call(deal, outs, (me_y, packed), 2 * SLOTS * SLOTS * pre_width)
    pre_rows, ring_tokens = lax.optimization_barrier((pre_rows, ring_tokens))
    pre_rows = lax.all_to_all(pre_rows.reshape(RING_SIZE, COLS * CAP, pre_width), RING, 0, 0, tiled=True)
    pre_rows = pre_rows.reshape(SLOTS, pre_width)

    weigh = functools.partial(weigh_kernel, tok=tok, topk=topk)
    outs = [out((per_col, width), bf16)] * COLS
    at = jnp.concatenate([me_y, me_z])
    sent = call(weigh, outs, (at, ring_tokens.astype(bf16)), 2 * SLOTS * tok * RING_SIZE * width)
    came = [sent[0]]
    for hop in range(1, COLS):
        came.append(lax.ppermute(sent[hop], "y", [(col, (col + hop) % COLS) for col in range(COLS)]))
    outs = [out((SLOTS, width), bf16)]
    (weight_rows,) = call(gather_kernel, outs, (me_y, *came), 2 * SLOTS * SLOTS * width)

    outs = [out((SLOTS, width + FACTS), bf16), out((SLOTS, hidden_width), bf16)]
    inputs = (weight_rows, pre_rows, w_gate[0], w_up[0], w_down[0])
    back, hidden = call(expert_kernel, outs, inputs, 6 * SLOTS * hidden_width * width)
    partial = dot(hidden, weight_rows, (0, 0)).astype(bf16)
    d_down = lax.psum_scatter(partial, "dp", scatter_dimension=0, tiled=True)
    back = lax.all_to_all(back.reshape(RING_SIZE, COLS * CAP, width + FACTS), RING, 0, 0, tiled=True)
    back = back.reshape(SLOTS, width + FACTS)

    join = functools.partial(join_kernel, topk=topk)
    home = [out((tokens, width + FACTS), bf16)]
    (home,) = call(join, home, (me_y, back, place, facts), 2 * tokens * SLOTS * width)
    home = lax.all_to_all(home.reshape(COLS, tok, width + FACTS), "y", 0, 0, tiled=True)
    outs = [out((tok, width), bf16), out((topk, tok), f32)]
    d_tokens, d_gates = call(finish_kernel, outs, (home, gates.T), COLS * tok * width)
    return (d_tokens, d_gates.T, d_down[None])


def solution(mesh):
    devices = mesh.devices
    dp, node, local = devices.shape
    split = Mesh(devices.reshape(dp, node, local // 2, 2), ("dp", "node", "y", "zh"))
    owner = ("dp", "node", "y", "zh")
    expert = ("node", "y", "zh")
    in_specs = (
        P(owner, None),
        P(owner, None, None),
        P(owner, None),
        P(owner, None),
        P(expert, None, None),
        P(expert, None, None),
        P(expert, None, None),
    )
    out_specs = (P(owner, None), P(owner, None), P(expert, "dp", None))
    return jax.shard_map(shards, mesh=split, in_specs=in_specs, out_specs=out_specs, check_vma=False)
```

```python
import functools

import jax
import jax.numpy as jnp
from jax import lax
from jax.experimental import pallas as pl
from jax.experimental.pallas import tpu as pltpu
from jax.sharding import Mesh, PartitionSpec as P

RING = ("zh", "node")
CAP = 2
COLS = 4
RING_SIZE = 32
HALF = RING_SIZE // 2
SLOTS = COLS * RING_SIZE * CAP
FACTS = 128
RAISES = (64, 32, 8, 4, 2, 1)
MIDDLE = 2.0**14
LOW = 2.0**20
VMEM_BYTES = 32 * 1024 * 1024
f32, bf16, i32 = jnp.float32, jnp.bfloat16, jnp.int32


def dot(left, right, contract=(1, 0)):
    dims = ((contract[:1], contract[1:]), ((), ()))
    return lax.dot_general(left, right, dims, preferred_element_type=f32)


def iota(shape, axis):
    return lax.broadcasted_iota(i32, shape, axis)


def expert_of(ring_index, column):
    return (ring_index % HALF) * 8 + column * 2 + ring_index // HALF


def one_hot(mask):
    return jnp.where(mask, 1.0, 0.0).astype(bf16)


def pack_kernel(routes_ref, gates_ref, grad_ref, pre_ref, out_ref, tokens_ref):
    topk, tok = routes_ref.shape
    routes_of, width = tok * topk, pre_ref.shape[1]
    per_col = RING_SIZE * CAP
    routes = routes_ref[...].astype(f32).astype(bf16)
    row_tok, row_k = iota((routes_of, tok), 0) // topk, iota((routes_of, topk), 0) % topk
    spread = dot(one_hot(row_tok == iota((routes_of, tok), 1)), routes, (1, 1))
    named = jnp.sum(jnp.where(row_k == iota((routes_of, topk), 1), spread, 0.0), axis=1, keepdims=True)
    slot = iota((routes_of, SLOTS), 1)
    wanted = expert_of(slot % per_col // CAP, slot // per_col).astype(f32)
    hit = one_hot(named == wanted)
    pair = (routes_of, routes_of)
    earlier = one_hot(iota(pair, 1) // topk < iota(pair, 0) // topk)
    before = dot(earlier, hit)
    pick = jnp.where(before == (slot % CAP).astype(f32), hit.astype(f32), 0.0).astype(bf16)
    rows = dot(pick, pre_ref[...], (0, 0)).astype(bf16)
    gates = gates_ref[...]
    high = gates.astype(bf16)
    rest = gates - high.astype(f32)
    middle = rest.astype(bf16)
    low = (rest - middle.astype(f32)).astype(bf16)
    seats = [one_hot(iota((topk, FACTS), 1) == iota((topk, FACTS), 0) + at * topk) for at in range(4)]
    named = dot(routes, seats[0], (0, 0))
    facts = named + dot(high, seats[1], (0, 0)) + dot(middle, seats[2], (0, 0)) * MIDDLE
    facts = facts + dot(low, seats[3], (0, 0)) * LOW
    grad = grad_ref[...].astype(f32)
    top = jnp.max(jnp.abs(grad), axis=1, keepdims=True)
    scale, raised = jnp.ones((tok, 1), f32), jnp.zeros((tok, 1), f32)
    for step in RAISES:
        fits = top * (scale * 2.0**step) <= 2.0**15
        scale = jnp.where(fits, scale * 2.0**step, scale)
        raised = jnp.where(fits, raised + step, raised)
    facts = jnp.where(iota((tok, FACTS), 1) == 4 * topk, raised, facts)
    tokens_ref[:, : grad.shape[1]] = grad * scale
    tokens_ref[:, grad.shape[1] :] = facts
    for col in range(COLS):
        out_ref[col, :per_col, :] = rows[col * per_col : (col + 1) * per_col]
        out_ref[col, per_col:, :FACTS] = named.astype(bf16)
        out_ref[col, per_col:, FACTS:] = jnp.zeros((tok, width - FACTS), bf16)


def deal_kernel(col_ref, in_ref, out_ref, place_ref, facts_ref, *, tok, topk):
    width = in_ref.shape[2]
    per_col = RING_SIZE * CAP
    tokens = COLS * tok
    me = col_ref[0]
    facts = in_ref[:, per_col:, :FACTS].reshape(tokens, FACTS)
    facts_ref[...] = facts
    square = (FACTS, FACTS)
    turned = dot(one_hot(iota(square, 0) == iota(square, 1)), facts, (1, 1))
    shape = (SLOTS, tokens)
    slot, token = iota(shape, 0), iota(shape, 1)
    wanted = expert_of(slot // (COLS * CAP), me).astype(f32)
    hit = jnp.zeros(shape, f32)
    for k in range(topk):
        hit = jnp.where(turned[k : k + 1] == wanted, 1.0, hit)
    pair = (tokens, tokens)
    first, second = iota(pair, 0), iota(pair, 1)
    earlier = jnp.where(first // tok == second // tok, jnp.where(first < second, 1.0, 0.0), 0.0).astype(bf16)
    before = dot(hit.astype(bf16), earlier)
    same = jnp.where(slot % (COLS * CAP) // CAP == token // tok, hit, 0.0)
    place = jnp.where(before == (slot % CAP).astype(f32), same, 0.0).astype(bf16)
    eye = one_hot(first == second)
    place_ref[...] = dot(eye, place, (1, 1)).astype(bf16)
    square = (SLOTS, SLOTS)
    slot = iota(square, 0)
    origin = slot % (COLS * CAP) // CAP * per_col + slot // (COLS * CAP) * CAP + slot % CAP
    swap = one_hot(origin == iota(square, 1))
    out_ref[...] = dot(swap, in_ref[:, :per_col, :].reshape(SLOTS, width)).astype(bf16)


def weigh_kernel(at_ref, in_ref, *out_refs, tok, topk):
    tokens = in_ref.shape[0]
    width = in_ref.shape[1] - FACTS
    me, place_me = at_ref[0], at_ref[1]
    square = (FACTS, FACTS)
    turned = dot(one_hot(iota(square, 0) == iota(square, 1)), in_ref[:, width:], (1, 1))
    routes = turned[:topk]
    gates = turned[topk : 2 * topk] + turned[2 * topk : 3 * topk] * (1.0 / MIDDLE)
    gates = gates + turned[3 * topk : 4 * topk] * (1.0 / LOW)
    raised = turned[4 * topk : 4 * topk + 1]
    lower = jnp.ones((1, tokens), f32)
    for step in RAISES:
        has = raised >= step
        lower = jnp.where(has, lower * 2.0**-step, lower)
        raised = jnp.where(has, raised - step, raised)
    hits, gate = [], []
    stack = jnp.zeros((8, tokens), f32)
    row = iota((8, tokens), 0)
    for col in range(COLS):
        wanted = expert_of(place_me, (me + col) % COLS).astype(f32)
        match = routes == wanted
        hits.append(jnp.sum(jnp.where(match, 1.0, 0.0), axis=0, keepdims=True))
        gate.append(jnp.sum(jnp.where(match, gates, 0.0), axis=0, keepdims=True))
        stack = jnp.where(row == col, hits[col], stack)
    pair = (tokens, tokens)
    first, second = iota(pair, 0), iota(pair, 1)
    earlier = jnp.where(first // tok == second // tok, jnp.where(first < second, 1.0, 0.0), 0.0).astype(bf16)
    before = dot(stack.astype(bf16), earlier)
    shape = (RING_SIZE * CAP, tokens)
    slot, token = iota(shape, 0), iota(shape, 1)
    for col in range(COLS):
        place = jnp.where(slot // CAP == token // tok, hits[col], 0.0)
        place = jnp.where(before[col : col + 1] == (slot % CAP).astype(f32), place, 0.0)
        scale = jnp.sum(place * gate[col], axis=1, keepdims=True)
        unit = jnp.sum(place * lower, axis=1, keepdims=True)
        rows = dot(place.astype(bf16), in_ref[:, :width]) * unit
        out_refs[col][...] = (rows * scale).astype(bf16)


def gather_kernel(col_ref, *refs):
    in_refs, out_ref = refs[:-1], refs[-1]
    me = col_ref[0]
    per_col = RING_SIZE * CAP
    shape = (SLOTS, per_col)
    slot = iota(shape, 0)
    column = slot % (COLS * CAP) // CAP
    origin = slot // (COLS * CAP) * CAP + slot % CAP
    total = jnp.zeros(out_ref.shape, f32)
    for hop, ref in enumerate(in_refs):
        away = (me - hop + COLS) % COLS
        picked = jnp.where(column == away, jnp.where(origin == iota(shape, 1), 1.0, 0.0), 0.0)
        total = total + dot(picked.astype(bf16), ref[...])
    out_ref[...] = total.astype(bf16)


def join_kernel(col_ref, back_ref, place_ref, facts_ref, out_ref, *, topk):
    tokens = place_ref.shape[0]
    width = out_ref.shape[1] - FACTS
    me = col_ref[0]
    place = place_ref[...]
    out_ref[:, :width] = dot(place, back_ref[:, :width]).astype(bf16)
    lane = (8, FACTS)
    head = one_hot(iota(lane, 1) == iota(lane, 0))
    dots = dot(head, back_ref[:, width:], (1, 1))[0:1]
    held = place.astype(f32) * dots
    shape = (tokens, SLOTS)
    expert = expert_of(iota(shape, 1) // (COLS * CAP), me).astype(f32)
    facts = facts_ref[...].astype(f32)
    lanes = iota((tokens, FACTS), 1)
    result = jnp.zeros((tokens, FACTS), f32)
    for k in range(topk):
        named = jnp.sum(jnp.where(lanes == k, facts, 0.0), axis=1, keepdims=True)
        value = jnp.sum(jnp.where(named == expert, held, 0.0), axis=1, keepdims=True)
        result = jnp.where(lanes == k, value, result)
    out_ref[:, width:] = result.astype(bf16)


def expert_kernel(rows_ref, pre_ref, gate_hbm, up_hbm, down_hbm, back_ref, hidden_ref, gate_ref, up_ref, down_ref, sems):
    moves = []
    for at, (source, target) in enumerate(((down_hbm, down_ref), (gate_hbm, gate_ref), (up_hbm, up_ref))):
        moves.append(pltpu.make_async_copy(source, target, sems.at[at]))
        moves[at].start()
    hidden_width = down_ref.shape[0]
    width = down_ref.shape[1]
    gate_pre = pre_ref[:, :hidden_width].astype(f32)
    up_pre = pre_ref[:, hidden_width:].astype(f32)
    sigmoid_gate = jax.nn.sigmoid(gate_pre)
    activated = gate_pre * sigmoid_gate
    hidden = (activated * up_pre).astype(bf16)
    hidden_ref[...] = hidden
    moves[0].wait()
    hidden_grad = dot(rows_ref[...], down_ref[...], (1, 1))
    dots = jnp.sum(hidden.astype(f32) * hidden_grad, axis=1, keepdims=True)
    lanes = iota((rows_ref.shape[0], FACTS), 1)
    back_ref[:, width:] = jnp.where(lanes == 0, dots, 0.0).astype(bf16)
    gate_grad = (hidden_grad * up_pre * sigmoid_gate * (1.0 + gate_pre * (1.0 - sigmoid_gate))).astype(bf16)
    up_grad = (hidden_grad * activated).astype(bf16)
    moves[1].wait()
    route_grad = dot(gate_grad, gate_ref[...], (1, 1))
    moves[2].wait()
    route_grad = route_grad + dot(up_grad, up_ref[...], (1, 1))
    back_ref[:, :width] = route_grad.astype(bf16)


def finish_kernel(home_ref, gates_ref, tokens_ref, gates_out_ref):
    width = tokens_ref.shape[1]
    topk = gates_ref.shape[0]
    total = home_ref[0].astype(f32)
    for col in range(1, COLS):
        total = total + home_ref[col].astype(f32)
    tokens_ref[...] = total[:, :width].astype(bf16)
    seat = one_hot(iota((topk, FACTS), 1) == iota((topk, FACTS), 0))
    gates_out_ref[...] = dot(seat, total[:, width:].astype(bf16), (1, 1)) / gates_ref[...]


def call(kernel, outs, inputs, flops, far=0, scratch=()):
    scalar = inputs[0].ndim == 1
    in_specs = [pl.BlockSpec(memory_space=pltpu.VMEM) for _ in inputs]
    if scalar:
        in_specs[0] = pl.BlockSpec(memory_space=pltpu.SMEM)
    for at in range(len(inputs) - far, len(inputs)):
        in_specs[at] = pl.BlockSpec(memory_space=pl.ANY)
    moved = sum(a.size * a.dtype.itemsize for a in inputs) + sum(a.size * a.dtype.itemsize for a in outs)
    return pl.pallas_call(
        kernel,
        out_shape=outs,
        in_specs=in_specs,
        out_specs=[pl.BlockSpec(memory_space=pltpu.VMEM) for _ in outs],
        scratch_shapes=list(scratch),
        compiler_params=pltpu.CompilerParams(vmem_limit_bytes=VMEM_BYTES),
        cost_estimate=pl.CostEstimate(flops=flops, bytes_accessed=moved, transcendentals=0),
    )(*inputs)


def shards(grad_out, saved_pre, gates, routes, w_gate, w_up, w_down):
    tok, topk = routes.shape
    width = grad_out.shape[1]
    pre_width = saved_pre.shape[2]
    hidden_width = pre_width // 2
    me_y = lax.axis_index("y").astype(i32).reshape(1)
    me_z = (lax.axis_index("zh") * HALF + lax.axis_index("node")).astype(i32).reshape(1)
    out = jax.ShapeDtypeStruct
    per_col = RING_SIZE * CAP
    tokens = COLS * tok

    pre = saved_pre.reshape(tok * topk, pre_width)
    outs = [out((COLS, per_col + tok, pre_width), bf16), out((tok, width + FACTS), f32)]
    inputs = (routes.T, gates.T, grad_out, pre)
    packed, own = call(pack_kernel, outs, inputs, 2 * SLOTS * tok * topk * pre_width)
    packed = lax.all_to_all(packed, "y", 0, 0, tiled=True)

    ring_tokens = lax.all_gather(own.astype(jnp.float16), RING, axis=0, tiled=True)
    outs = [out((SLOTS, pre_width), bf16), out((tokens, SLOTS), bf16), out((tokens, FACTS), bf16)]
    deal = functools.partial(deal_kernel, tok=tok, topk=topk)
    pre_rows, place, facts = call(deal, outs, (me_y, packed), 2 * SLOTS * SLOTS * pre_width)
    pre_rows, ring_tokens = lax.optimization_barrier((pre_rows, ring_tokens))
    pre_rows = lax.all_to_all(pre_rows.reshape(RING_SIZE, COLS * CAP, pre_width), RING, 0, 0, tiled=True)
    pre_rows = pre_rows.reshape(SLOTS, pre_width)

    weigh = functools.partial(weigh_kernel, tok=tok, topk=topk)
    outs = [out((per_col, width), bf16)] * COLS
    at = jnp.concatenate([me_y, me_z])
    sent = call(weigh, outs, (at, ring_tokens.astype(bf16)), 2 * SLOTS * tok * RING_SIZE * width)
    came = [sent[0]]
    for hop in range(1, COLS):
        came.append(lax.ppermute(sent[hop], "y", [(col, (col + hop) % COLS) for col in range(COLS)]))
    outs = [out((SLOTS, width), bf16)]
    (weight_rows,) = call(gather_kernel, outs, (me_y, *came), 2 * SLOTS * SLOTS * width)

    outs = [out((SLOTS, width + FACTS), bf16), out((SLOTS, hidden_width), bf16)]
    inputs = (weight_rows, pre_rows, w_gate[0], w_up[0], w_down[0])
    scratch = [pltpu.VMEM(w.shape, bf16) for w in inputs[2:]] + [pltpu.SemaphoreType.DMA((3,))]
    back, hidden = call(expert_kernel, outs, inputs, 6 * SLOTS * hidden_width * width, 3, scratch)
    partial = dot(hidden, weight_rows, (0, 0)).astype(bf16)
    d_down = lax.psum_scatter(partial, "dp", scatter_dimension=0, tiled=True)
    back = lax.all_to_all(back.reshape(RING_SIZE, COLS * CAP, width + FACTS), RING, 0, 0, tiled=True)
    back = back.reshape(SLOTS, width + FACTS)

    join = functools.partial(join_kernel, topk=topk)
    home = [out((tokens, width + FACTS), bf16)]
    (home,) = call(join, home, (me_y, back, place, facts), 2 * tokens * SLOTS * width)
    home = lax.all_to_all(home.reshape(COLS, tok, width + FACTS), "y", 0, 0, tiled=True)
    outs = [out((tok, width), bf16), out((topk, tok), f32)]
    d_tokens, d_gates = call(finish_kernel, outs, (home, gates.T), COLS * tok * width)
    return (d_tokens, d_gates.T, d_down[None])


def solution(mesh):
    devices = mesh.devices
    dp, node, local = devices.shape
    split = Mesh(devices.reshape(dp, node, local // 2, 2), ("dp", "node", "y", "zh"))
    owner = ("dp", "node", "y", "zh")
    expert = ("node", "y", "zh")
    in_specs = (
        P(owner, None),
        P(owner, None, None),
        P(owner, None),
        P(owner, None),
        P(expert, None, None),
        P(expert, None, None),
        P(expert, None, None),
    )
    out_specs = (P(owner, None), P(owner, None), P(expert, "dp", None))
    return jax.shard_map(shards, mesh=split, in_specs=in_specs, out_specs=out_specs, check_vma=False)
```

```python
import functools

import jax
import jax.numpy as jnp
from jax import lax
from jax.experimental import pallas as pl
from jax.experimental.pallas import tpu as pltpu
from jax.sharding import Mesh, PartitionSpec as P

RING = ("zh", "node")
CAP = 2
COLS = 4
RING_SIZE = 32
HALF = RING_SIZE // 2
SLOTS = COLS * RING_SIZE * CAP
FACTS = 128
RAISES = (64, 32, 8, 4, 2, 1)
MIDDLE = 2.0**14
LOW = 2.0**20
VMEM_BYTES = 32 * 1024 * 1024
f32, bf16, i32 = jnp.float32, jnp.bfloat16, jnp.int32


def dot(left, right, contract=(1, 0)):
    dims = ((contract[:1], contract[1:]), ((), ()))
    return lax.dot_general(left, right, dims, preferred_element_type=f32)


def iota(shape, axis):
    return lax.broadcasted_iota(i32, shape, axis)


def expert_of(ring_index, column):
    return (ring_index % HALF) * 8 + column * 2 + ring_index // HALF


def one_hot(mask):
    return jnp.where(mask, 1.0, 0.0).astype(bf16)


def pack_kernel(routes_ref, gates_ref, grad_ref, pre_ref, out_ref, tokens_ref):
    topk, tok = routes_ref.shape
    routes_of, width = tok * topk, pre_ref.shape[1]
    per_col = RING_SIZE * CAP
    routes = routes_ref[...].astype(f32).astype(bf16)
    row_tok, row_k = iota((routes_of, tok), 0) // topk, iota((routes_of, topk), 0) % topk
    spread = dot(one_hot(row_tok == iota((routes_of, tok), 1)), routes, (1, 1))
    named = jnp.sum(jnp.where(row_k == iota((routes_of, topk), 1), spread, 0.0), axis=1, keepdims=True)
    slot = iota((routes_of, SLOTS), 1)
    wanted = expert_of(slot % per_col // CAP, slot // per_col).astype(f32)
    hit = one_hot(named == wanted)
    pair = (routes_of, routes_of)
    earlier = one_hot(iota(pair, 1) // topk < iota(pair, 0) // topk)
    before = dot(earlier, hit)
    pick = jnp.where(before == (slot % CAP).astype(f32), hit.astype(f32), 0.0).astype(bf16)
    rows = dot(pick, pre_ref[...], (0, 0)).astype(bf16)
    gates = gates_ref[...]
    high = gates.astype(bf16)
    rest = gates - high.astype(f32)
    middle = rest.astype(bf16)
    low = (rest - middle.astype(f32)).astype(bf16)
    seats = [one_hot(iota((topk, FACTS), 1) == iota((topk, FACTS), 0) + at * topk) for at in range(4)]
    named = dot(routes, seats[0], (0, 0))
    facts = named + dot(high, seats[1], (0, 0)) + dot(middle, seats[2], (0, 0)) * MIDDLE
    facts = facts + dot(low, seats[3], (0, 0)) * LOW
    grad = grad_ref[...].astype(f32)
    top = jnp.max(jnp.abs(grad), axis=1, keepdims=True)
    scale, raised = jnp.ones((tok, 1), f32), jnp.zeros((tok, 1), f32)
    for step in RAISES:
        fits = top * (scale * 2.0**step) <= 2.0**15
        scale = jnp.where(fits, scale * 2.0**step, scale)
        raised = jnp.where(fits, raised + step, raised)
    facts = jnp.where(iota((tok, FACTS), 1) == 4 * topk, raised, facts)
    tokens_ref[:, : grad.shape[1]] = grad * scale
    tokens_ref[:, grad.shape[1] :] = facts
    for col in range(COLS):
        out_ref[col, :per_col, :] = rows[col * per_col : (col + 1) * per_col]
        out_ref[col, per_col:, :FACTS] = named.astype(bf16)
        out_ref[col, per_col:, FACTS:] = jnp.zeros((tok, width - FACTS), bf16)


def deal_kernel(col_ref, in_ref, out_ref, place_ref, facts_ref, *, tok, topk):
    width = in_ref.shape[2]
    per_col = RING_SIZE * CAP
    tokens = COLS * tok
    me = col_ref[0]
    facts = in_ref[:, per_col:, :FACTS].reshape(tokens, FACTS)
    facts_ref[...] = facts
    square = (FACTS, FACTS)
    turned = dot(one_hot(iota(square, 0) == iota(square, 1)), facts, (1, 1))
    shape = (SLOTS, tokens)
    slot, token = iota(shape, 0), iota(shape, 1)
    wanted = expert_of(slot // (COLS * CAP), me).astype(f32)
    hit = jnp.zeros(shape, f32)
    for k in range(topk):
        hit = jnp.where(turned[k : k + 1] == wanted, 1.0, hit)
    pair = (tokens, tokens)
    first, second = iota(pair, 0), iota(pair, 1)
    earlier = jnp.where(first // tok == second // tok, jnp.where(first < second, 1.0, 0.0), 0.0).astype(bf16)
    before = dot(hit.astype(bf16), earlier)
    same = jnp.where(slot % (COLS * CAP) // CAP == token // tok, hit, 0.0)
    place = jnp.where(before == (slot % CAP).astype(f32), same, 0.0).astype(bf16)
    eye = one_hot(first == second)
    place_ref[...] = dot(eye, place, (1, 1)).astype(bf16)
    square = (SLOTS, SLOTS)
    slot = iota(square, 0)
    origin = slot % (COLS * CAP) // CAP * per_col + slot // (COLS * CAP) * CAP + slot % CAP
    swap = one_hot(origin == iota(square, 1))
    out_ref[...] = dot(swap, in_ref[:, :per_col, :].reshape(SLOTS, width)).astype(bf16)


def weigh_kernel(at_ref, in_ref, *out_refs, tok, topk):
    tokens = in_ref.shape[0]
    width = in_ref.shape[1] - FACTS
    me, place_me = at_ref[0], at_ref[1]
    square = (FACTS, FACTS)
    turned = dot(one_hot(iota(square, 0) == iota(square, 1)), in_ref[:, width:], (1, 1))
    routes = turned[:topk]
    gates = turned[topk : 2 * topk] + turned[2 * topk : 3 * topk] * (1.0 / MIDDLE)
    gates = gates + turned[3 * topk : 4 * topk] * (1.0 / LOW)
    raised = turned[4 * topk : 4 * topk + 1]
    lower = jnp.ones((1, tokens), f32)
    for step in RAISES:
        has = raised >= step
        lower = jnp.where(has, lower * 2.0**-step, lower)
        raised = jnp.where(has, raised - step, raised)
    hits, gate = [], []
    stack = jnp.zeros((8, tokens), f32)
    row = iota((8, tokens), 0)
    for col in range(COLS):
        wanted = expert_of(place_me, (me + col) % COLS).astype(f32)
        match = routes == wanted
        hits.append(jnp.sum(jnp.where(match, 1.0, 0.0), axis=0, keepdims=True))
        gate.append(jnp.sum(jnp.where(match, gates, 0.0), axis=0, keepdims=True))
        stack = jnp.where(row == col, hits[col], stack)
    pair = (tokens, tokens)
    first, second = iota(pair, 0), iota(pair, 1)
    earlier = jnp.where(first // tok == second // tok, jnp.where(first < second, 1.0, 0.0), 0.0).astype(bf16)
    before = dot(stack.astype(bf16), earlier)
    shape = (RING_SIZE * CAP, tokens)
    slot, token = iota(shape, 0), iota(shape, 1)
    for col in range(COLS):
        place = jnp.where(slot // CAP == token // tok, hits[col], 0.0)
        place = jnp.where(before[col : col + 1] == (slot % CAP).astype(f32), place, 0.0)
        scale = jnp.sum(place * gate[col], axis=1, keepdims=True)
        unit = jnp.sum(place * lower, axis=1, keepdims=True)
        rows = dot(place.astype(bf16), in_ref[:, :width]) * unit
        out_refs[col][...] = (rows * scale).astype(bf16)


def gather_kernel(col_ref, *refs):
    in_refs, out_ref = refs[:-1], refs[-1]
    me = col_ref[0]
    per_col = RING_SIZE * CAP
    shape = (SLOTS, per_col)
    slot = iota(shape, 0)
    column = slot % (COLS * CAP) // CAP
    origin = slot // (COLS * CAP) * CAP + slot % CAP
    total = jnp.zeros(out_ref.shape, f32)
    for hop, ref in enumerate(in_refs):
        away = (me - hop + COLS) % COLS
        picked = jnp.where(column == away, jnp.where(origin == iota(shape, 1), 1.0, 0.0), 0.0)
        total = total + dot(picked.astype(bf16), ref[...])
    out_ref[...] = total.astype(bf16)


def join_kernel(col_ref, back_ref, place_ref, facts_ref, out_ref, *, topk):
    tokens = place_ref.shape[0]
    width = out_ref.shape[1] - FACTS
    me = col_ref[0]
    place = place_ref[...]
    out_ref[:, :width] = dot(place, back_ref[:, :width]).astype(bf16)
    lane = (8, FACTS)
    head = one_hot(iota(lane, 1) == iota(lane, 0))
    dots = dot(head, back_ref[:, width:], (1, 1))[0:1]
    held = place.astype(f32) * dots
    shape = (tokens, SLOTS)
    expert = expert_of(iota(shape, 1) // (COLS * CAP), me).astype(f32)
    facts = facts_ref[...].astype(f32)
    lanes = iota((tokens, FACTS), 1)
    result = jnp.zeros((tokens, FACTS), f32)
    for k in range(topk):
        named = jnp.sum(jnp.where(lanes == k, facts, 0.0), axis=1, keepdims=True)
        value = jnp.sum(jnp.where(named == expert, held, 0.0), axis=1, keepdims=True)
        result = jnp.where(lanes == k, value, result)
    out_ref[:, width:] = result.astype(bf16)


def expert_kernel(rows_ref, pre_ref, gate_hbm, up_hbm, down_hbm, back_ref, hidden_ref, gate_ref, up_ref, down_ref, sems):
    moves = []
    for at, (source, target) in enumerate(((down_hbm, down_ref), (gate_hbm, gate_ref), (up_hbm, up_ref))):
        moves.append(pltpu.make_async_copy(source, target, sems.at[at]))
        moves[at].start()
    hidden_width = down_ref.shape[0]
    width = down_ref.shape[1]
    gate_pre = pre_ref[:, :hidden_width].astype(f32)
    up_pre = pre_ref[:, hidden_width:].astype(f32)
    sigmoid_gate = jax.nn.sigmoid(gate_pre)
    activated = gate_pre * sigmoid_gate
    hidden = (activated * up_pre).astype(bf16)
    hidden_ref[...] = hidden
    moves[0].wait()
    hidden_grad = dot(rows_ref[...], down_ref[...], (1, 1))
    dots = jnp.sum(hidden.astype(f32) * hidden_grad, axis=1, keepdims=True)
    lanes = iota((rows_ref.shape[0], FACTS), 1)
    back_ref[:, width:] = jnp.where(lanes == 0, dots, 0.0).astype(bf16)
    gate_grad = (hidden_grad * up_pre * sigmoid_gate * (1.0 + gate_pre * (1.0 - sigmoid_gate))).astype(bf16)
    up_grad = (hidden_grad * activated).astype(bf16)
    moves[1].wait()
    route_grad = dot(gate_grad, gate_ref[...], (1, 1))
    moves[2].wait()
    route_grad = route_grad + dot(up_grad, up_ref[...], (1, 1))
    back_ref[:, :width] = route_grad.astype(bf16)


def finish_kernel(home_ref, gates_ref, tokens_ref, gates_out_ref):
    width = tokens_ref.shape[1]
    topk = gates_ref.shape[0]
    total = home_ref[0].astype(f32)
    for col in range(1, COLS):
        total = total + home_ref[col].astype(f32)
    tokens_ref[...] = total[:, :width].astype(bf16)
    seat = one_hot(iota((topk, FACTS), 1) == iota((topk, FACTS), 0))
    gates_out_ref[...] = dot(seat, total[:, width:].astype(bf16), (1, 1)) / gates_ref[...]


def call(kernel, outs, inputs, flops, far=0, scratch=()):
    scalar = inputs[0].ndim == 1
    in_specs = [pl.BlockSpec(memory_space=pltpu.VMEM) for _ in inputs]
    if scalar:
        in_specs[0] = pl.BlockSpec(memory_space=pltpu.SMEM)
    for at in range(len(inputs) - far, len(inputs)):
        in_specs[at] = pl.BlockSpec(memory_space=pltpu.HBM)
    moved = sum(a.size * a.dtype.itemsize for a in inputs) + sum(a.size * a.dtype.itemsize for a in outs)
    return pl.pallas_call(
        kernel,
        out_shape=outs,
        in_specs=in_specs,
        out_specs=[pl.BlockSpec(memory_space=pltpu.VMEM) for _ in outs],
        scratch_shapes=list(scratch),
        compiler_params=pltpu.CompilerParams(vmem_limit_bytes=VMEM_BYTES),
        cost_estimate=pl.CostEstimate(flops=flops, bytes_accessed=moved, transcendentals=0),
    )(*inputs)


def shards(grad_out, saved_pre, gates, routes, w_gate, w_up, w_down):
    tok, topk = routes.shape
    width = grad_out.shape[1]
    pre_width = saved_pre.shape[2]
    hidden_width = pre_width // 2
    me_y = lax.axis_index("y").astype(i32).reshape(1)
    me_z = (lax.axis_index("zh") * HALF + lax.axis_index("node")).astype(i32).reshape(1)
    out = jax.ShapeDtypeStruct
    per_col = RING_SIZE * CAP
    tokens = COLS * tok

    pre = saved_pre.reshape(tok * topk, pre_width)
    outs = [out((COLS, per_col + tok, pre_width), bf16), out((tok, width + FACTS), f32)]
    inputs = (routes.T, gates.T, grad_out, pre)
    packed, own = call(pack_kernel, outs, inputs, 2 * SLOTS * tok * topk * pre_width)
    packed = lax.all_to_all(packed, "y", 0, 0, tiled=True)

    ring_tokens = lax.all_gather(own.astype(jnp.float16), RING, axis=0, tiled=True)
    outs = [out((SLOTS, pre_width), bf16), out((tokens, SLOTS), bf16), out((tokens, FACTS), bf16)]
    deal = functools.partial(deal_kernel, tok=tok, topk=topk)
    pre_rows, place, facts = call(deal, outs, (me_y, packed), 2 * SLOTS * SLOTS * pre_width)
    pre_rows, ring_tokens = lax.optimization_barrier((pre_rows, ring_tokens))
    pre_rows = lax.all_to_all(pre_rows.reshape(RING_SIZE, COLS * CAP, pre_width), RING, 0, 0, tiled=True)
    pre_rows = pre_rows.reshape(SLOTS, pre_width)

    weigh = functools.partial(weigh_kernel, tok=tok, topk=topk)
    outs = [out((per_col, width), bf16)] * COLS
    at = jnp.concatenate([me_y, me_z])
    sent = call(weigh, outs, (at, ring_tokens.astype(bf16)), 2 * SLOTS * tok * RING_SIZE * width)
    came = [sent[0]]
    for hop in range(1, COLS):
        came.append(lax.ppermute(sent[hop], "y", [(col, (col + hop) % COLS) for col in range(COLS)]))
    outs = [out((SLOTS, width), bf16)]
    (weight_rows,) = call(gather_kernel, outs, (me_y, *came), 2 * SLOTS * SLOTS * width)

    outs = [out((SLOTS, width + FACTS), bf16), out((SLOTS, hidden_width), bf16)]
    inputs = (weight_rows, pre_rows, w_gate[0], w_up[0], w_down[0])
    scratch = [pltpu.VMEM(w.shape, bf16) for w in inputs[2:]] + [pltpu.SemaphoreType.DMA((3,))]
    back, hidden = call(expert_kernel, outs, inputs, 6 * SLOTS * hidden_width * width, 3, scratch)
    partial = dot(hidden, weight_rows, (0, 0)).astype(bf16)
    d_down = lax.psum_scatter(partial, "dp", scatter_dimension=0, tiled=True)
    back = lax.all_to_all(back.reshape(RING_SIZE, COLS * CAP, width + FACTS), RING, 0, 0, tiled=True)
    back = back.reshape(SLOTS, width + FACTS)

    join = functools.partial(join_kernel, topk=topk)
    home = [out((tokens, width + FACTS), bf16)]
    (home,) = call(join, home, (me_y, back, place, facts), 2 * tokens * SLOTS * width)
    home = lax.all_to_all(home.reshape(COLS, tok, width + FACTS), "y", 0, 0, tiled=True)
    outs = [out((tok, width), bf16), out((topk, tok), f32)]
    d_tokens, d_gates = call(finish_kernel, outs, (home, gates.T), COLS * tok * width)
    return (d_tokens, d_gates.T, d_down[None])


def solution(mesh):
    devices = mesh.devices
    dp, node, local = devices.shape
    split = Mesh(devices.reshape(dp, node, local // 2, 2), ("dp", "node", "y", "zh"))
    owner = ("dp", "node", "y", "zh")
    expert = ("node", "y", "zh")
    in_specs = (
        P(owner, None),
        P(owner, None, None),
        P(owner, None),
        P(owner, None),
        P(expert, None, None),
        P(expert, None, None),
        P(expert, None, None),
    )
    out_specs = (P(owner, None), P(owner, None), P(expert, "dp", None))
    return jax.shard_map(shards, mesh=split, in_specs=in_specs, out_specs=out_specs, check_vma=False)
```
